512 devices in a mesh: seq: 4 (over y), exp: 128 (over z, x, core).
Axes of the slice: x: 4, y: 4, z: 16, core: 2. Of those that a mesh axis runs over, the one named last changes fastest.
Arguments:
- states: bfloat16 [65536, 2048], P(('seq', 'exp')), may hold values from -6 to 6
- queries: bfloat16 [65536, 2048], P(('seq', 'exp')), may hold values from -36 to 36
- mem_keys: bfloat16 [256, 2048], P('seq'), may hold values from -4.1 to 4.1
- mem_values: bfloat16 [256, 2048], P('seq'), may hold values from -6 to 6
- expert_ids: int32 [65536], P(('seq', 'exp')), may hold values from 0 to 127, as said below
- send_counts: int32 [512, 4], P(('seq', 'exp')), may hold values from 0 to 2, as said below
- w_in: bfloat16 [4, 10240, 2048], P('seq', 'exp'), may hold values from -0.125 to 0.125
- w_out: bfloat16 [4, 10240, 2048], P('seq', 'exp'), may hold values from -0.125 to 0.125
- upstream: bfloat16 [65536, 2048], P(('seq', 'exp')), may hold values from -6 to 6
Outputs:
- grad_states: bfloat16 [65536, 2048], P(('seq', 'exp'))
- grad_queries: bfloat16 [65536, 2048], P(('seq', 'exp'))
- grad_keys: bfloat16 [256, 2048], P('seq')
- grad_values: bfloat16 [256, 2048], P('seq')
- grad_w_in: bfloat16 [4, 10240, 2048], P('seq', 'exp')
- grad_w_out: bfloat16 [4, 10240, 2048], P('seq', 'exp')
The draws below stay inside these ranges and needn't reach their ends.
Inputs may be any that keep to these rules, and one draw needn't show every extreme that they name: `expert_ids`: for each window expert (0 to 3) the tokens of one device name it at most 2 times, and the tokens of the 4 devices with one index of exp name it at most 2 times together; in every such group some window expert is named 2 times by one device. send_counts[b, e] is the number of tokens of device block b whose expert is window expert e.
All inputs are finite; a program needn't handle non-finite values.
Results may differ from the reference program's by a relative error of at most 0.0063.
Values may be sent and summed in bfloat16 or wider, within the bound.
No kernel may reach another device: no remote copies, remote signals or barrier semaphores. Data moves between devices by JAX's collectives and lax.ppermute only.
A program may use at most 64 MiB of HBM per device.

```python
import math
import jax
import jax.numpy as jnp
from jax import lax

D = 2048
HEAD = 64
FF = 10240
EXPERTS = 128
TOK_DEV = 128
GCAP = 2
WIN = 4
BLOCKS = 512
TOKENS = 65536
MEM = 256
N_SEQ = 4
N_EXP = 128


def routing(key):
    hot = jax.random.randint(jax.random.fold_in(key, 11), (N_EXP,), 0, N_SEQ)
    where_to = jax.random.randint(jax.random.fold_in(key, 12), (N_EXP, N_SEQ, 2), 0, N_SEQ)
    active = jax.random.randint(jax.random.fold_in(key, 13), (N_EXP, N_SEQ, 2), 0, 2)
    is_hot = jnp.arange(N_SEQ, dtype=jnp.int32)[None, :] == hot[:, None]
    second = jnp.where(is_hot, where_to[:, :, 0], where_to[:, :, 1])
    where_to = jnp.stack([where_to[:, :, 0], second], axis=2)
    active = jnp.where(is_hot[:, :, None], 1, active).astype(jnp.int32)
    hits = (where_to[:, :, :, None] == jnp.arange(N_SEQ, dtype=jnp.int32)[None, None, None, :]).astype(jnp.int32)
    tally = jnp.sum(hits * active[:, :, :, None], axis=2)
    tally = jnp.transpose(tally, (2, 0, 1)).reshape(BLOCKS, N_SEQ).astype(jnp.int32)

    def one_block(index, row_counts):
        block_key = jax.random.fold_in(jax.random.fold_in(key, 14), index)
        first_key, second_key = jax.random.split(block_key)
        bounds = jnp.cumsum(row_counts).astype(jnp.int32)
        places = jnp.arange(TOK_DEV, dtype=jnp.int32)
        window_id = jnp.sum((places[:, None] >= bounds[None, :]).astype(jnp.int32), axis=1)
        others = jax.random.randint(first_key, (TOK_DEV,), N_SEQ, EXPERTS)
        chosen = jnp.where(places < bounds[-1], window_id, others).astype(jnp.int32)
        return jax.random.permutation(second_key, chosen)
    chosen = jax.vmap(one_block)(jnp.arange(BLOCKS, dtype=jnp.int32), tally)
    return (chosen.reshape(-1), tally)


def memory_uniform(key):
    return jax.random.uniform(key, (MEM, D), jnp.float32, 1e-06, 1.0 - 1e-06)


def draw_expert_ids(key, part):
    chosen, tally = routing(key)
    return chosen


def draw_send_counts(key, part):
    chosen, tally = routing(key)
    return tally


def draw_mem_keys(key, part):
    base = memory_uniform(key)
    return jnp.clip(0.55 * (jnp.log(base) - jnp.log1p(-base)), -4.0, 4.0).astype(jnp.bfloat16)


def draw_queries(key, part):
    key = jax.random.fold_in(key, 4)
    return jnp.clip(jax.random.normal(key, (TOKENS, D), jnp.float32), -5.0, 5.0).astype(jnp.bfloat16)


def steps_of(own_key, extent, cuts, smallest, high):
    factor_of = 1.0
    for dim, shards_of in cuts:
        steps = jax.random.uniform(jax.random.fold_in(jax.random.fold_in(own_key, 6), dim), (shards_of,), jnp.float32, smallest / len(cuts), high / len(cuts))
        factor_of = factor_of * jnp.repeat(jnp.exp(steps), extent[dim] // shards_of).reshape((-1,) + (1,) * (len(extent) - 1 - dim))
    return factor_of


def bell_draw(stream_key, extent, deviation, bound, pieces=(), kind=jnp.bfloat16):
    values = deviation * jax.random.normal(stream_key, extent, jnp.float32)
    if pieces:
        values = values * steps_of(stream_key, extent, pieces, -0.22, 0.18)
    return jnp.clip(values, -bound, bound).astype(kind)


def setup_inputs(seed: int = 0) -> dict:
    arg_keys = jax.random.split(jax.random.key(seed), 10)
    return {
        "states": bell_draw(arg_keys[0], (TOKENS, D), 1.0, 6.0, ((0, 512),)),
        "queries": draw_queries(jax.random.fold_in(arg_keys[9], 71), 0),
        "mem_keys": draw_mem_keys(jax.random.fold_in(arg_keys[9], 71), 0),
        "mem_values": bell_draw(arg_keys[3], (MEM, D), 1.0, 6.0, ((0, 4),)),
        "expert_ids": draw_expert_ids(jax.random.fold_in(arg_keys[9], 71), 0),
        "send_counts": draw_send_counts(jax.random.fold_in(arg_keys[9], 71), 0),
        "w_in": bell_draw(arg_keys[6], (WIN, FF, D), D ** -0.5, 0.125, ((0, 4), (1, 128))),
        "w_out": bell_draw(arg_keys[7], (WIN, FF, D), D ** -0.5, 0.125, ((0, 4), (1, 128))),
        "upstream": bell_draw(arg_keys[8], (TOKENS, D), 1.0, 6.0, ((0, 512),)),
    }


def gelu_grad(pre, d_act):
    _, pullback = jax.vjp(jax.nn.gelu, pre)
    return pullback(d_act)[0]

def reference(states, queries, mem_keys, mem_values, expert_ids, send_counts, w_in, w_out, upstream):
    score_scale = HEAD ** (-0.5)
    row_total = states.shape[0]
    hidden_width = states.shape[1]
    head_count = hidden_width // HEAD
    mem_total = mem_keys.shape[0]
    key_per_head = mem_keys.reshape(mem_total, head_count, HEAD).astype(jnp.float32)
    value_per_head = mem_values.reshape(mem_total, head_count, HEAD).astype(jnp.float32)
    memory_extent = math.gcd(row_total, 4096)
    block_count = row_total // memory_extent

    def probabilities(query_block):
        query_per_head = query_block.reshape(memory_extent, head_count, HEAD).astype(jnp.float32)
        attention_scores = jnp.einsum('zyk,cyk->yzc', query_per_head, key_per_head) * score_scale
        return jax.nn.softmax(attention_scores, axis=-1)

    def rounded(values):
        return lax.optimization_barrier(values.astype(jnp.bfloat16)).astype(jnp.float32)

    def forward(query_block):
        attention_weights = rounded(probabilities(query_block))
        return jnp.einsum('fae,efb->afb', attention_weights, value_per_head).reshape(memory_extent, hidden_width)
    attended_values = lax.map(forward, queries.reshape(block_count, memory_extent, hidden_width)).reshape(row_total, hidden_width)
    mixed = (states.astype(jnp.float32) + attended_values).astype(jnp.bfloat16)
    device_count = row_total // TOK_DEV
    grouped = expert_ids.reshape(device_count, TOK_DEV)
    inside = grouped < N_SEQ
    expert = jnp.where(inside, grouped, 0).astype(jnp.int32)
    onehot = ((expert[:, :, None] == jnp.arange(N_SEQ, dtype=jnp.int32)[None, None, :]) & inside[:, :, None]).astype(jnp.int32)
    rank = lax.optimization_barrier(jnp.sum((jnp.cumsum(onehot, axis=1).astype(jnp.int32) - 1) * onehot, axis=2)).astype(jnp.int32)
    limit = jnp.take_along_axis(send_counts, expert, axis=1)
    group_counts = send_counts.reshape(N_SEQ, N_EXP, N_SEQ)
    offsets = (jnp.cumsum(group_counts, axis=0).astype(jnp.int32) - group_counts).reshape(device_count, N_SEQ)
    offset = jnp.take_along_axis(offsets, expert, axis=1)
    group = (jnp.arange(device_count, dtype=jnp.int32) % N_EXP)[:, None]
    position = (offset + rank).astype(jnp.int32)
    kept = inside & (rank < limit) & (position < GCAP)
    row_count = N_EXP * GCAP
    dummy = N_SEQ * row_count
    target = jnp.where(kept, expert * row_count + group * GCAP + position, dummy).reshape(-1).astype(jnp.int32)
    rows_all = jax.ops.segment_sum(mixed.astype(jnp.float32), target, num_segments=dummy + 1)[:dummy]
    grads_all = jax.ops.segment_sum(upstream.astype(jnp.float32), target, num_segments=dummy + 1)[:dummy]
    rows_all = rows_all.reshape(N_SEQ, row_count, hidden_width).astype(jnp.bfloat16)
    grads_all = grads_all.reshape(N_SEQ, row_count, hidden_width).astype(jnp.bfloat16)

    def expert_step(carry, inputs):
        rows, grads, weight_in, weight_out = inputs
        pre = jnp.dot(rows, weight_in.T, preferred_element_type=jnp.float32)
        act_b = jax.nn.gelu(pre).astype(jnp.bfloat16)
        d_act = jnp.dot(grads, weight_out.T, preferred_element_type=jnp.float32)
        d_pre = gelu_grad(pre, d_act).astype(jnp.bfloat16)
        g_in = jnp.dot(d_pre.T, rows, preferred_element_type=jnp.float32).astype(jnp.bfloat16)
        g_out = jnp.dot(act_b.T, grads, preferred_element_type=jnp.float32).astype(jnp.bfloat16)
        back = jnp.dot(d_pre, weight_in, preferred_element_type=jnp.float32).astype(jnp.bfloat16)
        return (carry, (back, g_in, g_out))
    _, (backs, grad_w_in, grad_w_out) = lax.scan(expert_step, jnp.zeros((), jnp.float32), (rows_all, grads_all, w_in, w_out))
    back_flat = jnp.concatenate([backs.reshape(dummy, hidden_width), jnp.zeros((1, hidden_width), jnp.bfloat16)], axis=0)
    moe_grad = back_flat[target]
    grad_states = (upstream.astype(jnp.float32) + moe_grad.astype(jnp.float32)).astype(jnp.bfloat16)

    def backward(total, inputs):
        query_block, grad_block = inputs
        probs = probabilities(query_block)
        attention_weights = rounded(probs)
        query_per_head = query_block.reshape(memory_extent, head_count, HEAD).astype(jnp.float32)
        gradient_per_head = grad_block.reshape(memory_extent, head_count, HEAD).astype(jnp.float32)
        probability_gradient = jnp.einsum('zyk,cyk->yzc', gradient_per_head, value_per_head)
        centre = lax.optimization_barrier(jnp.sum(probs * probability_gradient, axis=-1, keepdims=True))
        score_gradient = rounded(probs * (probability_gradient - centre) * score_scale)
        query_gradient = jnp.einsum('fae,efb->afb', score_gradient, key_per_head).reshape(memory_extent, hidden_width).astype(jnp.bfloat16)
        key_gradient = jnp.einsum('vro,rvx->ovx', score_gradient, query_per_head)
        value_gradient = jnp.einsum('vro,rvx->ovx', attention_weights, gradient_per_head)
        return ((total[0] + key_gradient, total[1] + value_gradient), query_gradient)
    empty = jnp.zeros((mem_total, head_count, HEAD), jnp.float32)
    (key_sum, value_sum), query_grads = lax.scan(backward, (empty, empty), (queries.reshape(block_count, memory_extent, hidden_width), grad_states.reshape(block_count, memory_extent, hidden_width)))
    grad_queries = query_grads.reshape(row_total, hidden_width)
    grad_keys = key_sum.reshape(mem_total, hidden_width).astype(jnp.bfloat16)
    grad_values = value_sum.reshape(mem_total, hidden_width).astype(jnp.bfloat16)
    return (grad_states, grad_queries, grad_keys, grad_values, grad_w_in, grad_w_out)
```

```python
import functools

import jax
import jax.numpy as jnp
from jax import lax
from jax.experimental import pallas as pl
from jax.experimental.pallas import tpu as pltpu
from jax.sharding import Mesh, PartitionSpec as P

HEAD = 64
GCAP = 2
SCALE = HEAD ** (-0.5)
BF, F32 = jnp.bfloat16, jnp.float32
DEVICES = ("y", "z", "x", "c")
PLANE = ("z", "x", "c")


def dot(left, right, left_dim=1, right_dim=0):
    return lax.dot_general(
        left, right, (((left_dim,), (right_dim,)), ((), ())), preferred_element_type=F32
    )


def exchange(values, axes):
    return lax.all_to_all(values, axes, split_axis=0, concat_axis=0, tiled=True)


def spread(values, axis):
    n = lax.axis_size(axis)
    copies = jnp.broadcast_to(values[None], (n,) + values.shape).reshape(
        (n * values.shape[0],) + values.shape[1:]
    )
    return exchange(copies, axis)


def collect(values, axes):
    n = lax.axis_size(axes)
    got = exchange(values, axes)
    return jnp.sum(got.reshape((n, -1) + got.shape[1:]).astype(F32), axis=0)


def other_core(values):
    return lax.ppermute(values, "c", [(0, 1), (1, 0)])


def attention_backward_kernel(
    core_ref, place_ref, rows_ref, up_ref, q_ref, k_ref, v_ref, gs_ref, gq_ref, keep_ref, send_ref
):
    first = core_ref[0] == 0
    moe = dot(place_ref[...], rows_ref[...])
    gs_ref[...] = (up_ref[...].astype(F32) + moe).astype(BF)
    tokens = q_ref.shape[0]
    low = lax.broadcasted_iota(jnp.int32, (tokens, 2 * HEAD), 1) < HEAD

    def both(block):
        none = jnp.zeros_like(block)
        return jnp.concatenate([jnp.where(low, block, none), jnp.where(low, none, block)], axis=0)

    for pair in range(q_ref.shape[1] // (2 * HEAD)):
        cols = slice(pair * 2 * HEAD, (pair + 1) * 2 * HEAD)
        queries = both(q_ref[:, cols] * BF(SCALE))
        grads = both(gs_ref[:, cols])
        keys, values = k_ref[:, cols], v_ref[:, cols]
        scores = dot(keys, queries, 1, 1)
        exps = jnp.exp(scores - jnp.max(scores, axis=0, keepdims=True))
        probs = exps * (1.0 / jnp.sum(exps, axis=0, keepdims=True))
        d_probs = dot(values, grads, 1, 1)
        centre = jnp.sum(probs * d_probs, axis=0, keepdims=True)
        d_scores = (probs * (d_probs - centre)).astype(BF)
        g_keys = dot(d_scores, queries)
        g_values = dot(probs.astype(BF), grads)
        keep_ref[:, cols] = jnp.where(first, g_keys, g_values).astype(BF)
        send_ref[:, cols] = jnp.where(first, g_values, g_keys).astype(BF)
        g_queries = dot(keys, d_scores, 0, 0)
        g_queries = jnp.concatenate([g_queries[:HEAD, :tokens], g_queries[HEAD:, tokens:]], axis=0)
        gq_ref[:, cols] = (g_queries.T * SCALE).astype(BF)


def attention_backward(core, place, rows, upstream, queries, keys, values):
    tokens, width = queries.shape
    mem = keys.shape[0]
    block = 512
    column = lambda n: pl.BlockSpec((n, block), lambda i: (0, i))
    return pl.pallas_call(
        attention_backward_kernel,
        grid=(width // block,),
        in_specs=[
            pl.BlockSpec(memory_space=pltpu.SMEM),
            pl.BlockSpec(place.shape, lambda i: (0, 0)),
            column(rows.shape[0]),
            column(tokens),
            column(tokens),
            column(mem),
            column(mem),
        ],
        out_specs=[column(tokens), column(tokens), column(mem), column(mem)],
        out_shape=[
            jax.ShapeDtypeStruct((tokens, width), BF),
            jax.ShapeDtypeStruct((tokens, width), BF),
            jax.ShapeDtypeStruct((mem, width), BF),
            jax.ShapeDtypeStruct((mem, width), BF),
        ],
        cost_estimate=pl.CostEstimate(
            flops=12 * tokens * mem * width, bytes_accessed=8 * mem * width, transcendentals=0
        ),
    )(core, place, rows, upstream, queries, keys, values)


def per_device(
    states, queries, mem_keys, mem_values, expert_ids, send_counts, w_in, w_out, upstream
):
    tokens, width = states.shape
    heads = width // HEAD
    window = lax.axis_size("y")
    slots = window * GCAP
    mine, core = lax.axis_index("y"), lax.axis_index("c")
    all_keys = lax.all_gather(mem_keys, "y", axis=0, tiled=True)
    all_values = lax.all_gather(mem_values, "y", axis=0, tiled=True)

    experts = jnp.arange(window, dtype=jnp.int32)
    onehot = (expert_ids[:, None] == experts[None, :]).astype(jnp.int32)
    rank = jnp.sum((jnp.cumsum(onehot, axis=0) - 1) * onehot, axis=1)
    limit = jnp.sum(onehot * send_counts, axis=1)
    slot = jnp.where(rank < limit, expert_ids * GCAP + rank, -1)
    slot_ids = jnp.arange(slots, dtype=jnp.int32)
    place = (slot_ids[:, None] == slot[None, :]).astype(BF)
    payload = [dot(place, part).astype(BF) for part in (queries, states, upstream)]
    flags = jnp.broadcast_to(jnp.repeat(send_counts[0], GCAP).astype(BF)[:, None], (slots, 128))
    group = lax.all_gather(jnp.concatenate(payload + [flags], axis=1), "y", axis=0, tiled=True)

    counts = group[:, 3 * width].reshape(window, slots)[:, ::GCAP].astype(jnp.int32)
    offsets = jnp.cumsum(counts, axis=0).astype(jnp.int32) - counts
    order = jnp.arange(GCAP, dtype=jnp.int32)
    position = offsets[:, :, None] + order
    kept = (order < counts[:, :, None]) & (position < GCAP)
    target = jnp.where(kept, experts[None, :, None] * GCAP + position, -1).reshape(-1)
    pack = (slot_ids[:, None] == target[None, :]).astype(BF)
    filled = jnp.sum(pack.astype(F32), axis=1)
    routed = dot(pack, group[:, : 3 * width]).astype(BF)
    own_target = lax.dynamic_slice_in_dim(target, mine * slots, slots, 0)
    own = (own_target[:, None] == slot_ids[None, :]).astype(BF)
    place_back = dot(place, own, 0, 0).astype(BF)

    in_head = jnp.arange(heads)[:, None] == (jnp.arange(width) // HEAD)[None, :]
    by_head = jnp.where(in_head[:, None, :], routed[None, :, :width], 0).reshape(-1, width)
    scores = dot(by_head, mem_keys, 1, 1) * SCALE
    top = jnp.max(scores, axis=1, keepdims=True)
    exps = jnp.exp(scores - top)
    total = jnp.sum(exps, axis=1)
    part = dot(exps.astype(BF), mem_values).reshape(heads, slots, width)
    part = jnp.sum(jnp.where(in_head[:, None, :], part, 0.0), axis=0)
    tops, totals = top.reshape(heads, slots).T, total.reshape(heads, slots).T
    pad = jnp.zeros((slots, 128 - 2 * heads), F32)
    parts = exchange(jnp.concatenate([part, tops, totals, pad], axis=1), "y")
    parts = parts.reshape(window, GCAP, -1)
    tops, totals = parts[:, :, width : width + heads], parts[:, :, width + heads : width + 2 * heads]
    share = jnp.exp(tops - jnp.max(tops, axis=0))
    share = share / jnp.sum(share * totals, axis=0)
    share = jnp.dot(
        share.reshape(-1, heads), in_head.astype(F32), precision=lax.Precision.HIGHEST
    ).reshape(window, GCAP, width)
    attended = jnp.sum(parts[:, :, :width] * share, axis=0)
    here = lax.dynamic_slice_in_dim(routed, mine * GCAP, GCAP, 0)
    here_filled = lax.dynamic_slice_in_dim(filled, mine * GCAP, GCAP, 0)
    row = (here[:, width : 2 * width].astype(F32) + attended) * here_filled[:, None]
    pair = jnp.concatenate([row.astype(BF), here[:, 2 * width :]], axis=1)

    near = spread(spread(pair, "z"), "x")
    far = other_core(near)
    weight_in, weight_out = w_in[0], w_out[0]

    def expert(block):
        rows, grads = block[:, :width], block[:, width:]
        pre = dot(rows, weight_in, 1, 1)
        act, pullback = jax.vjp(jax.nn.gelu, pre)
        d_pre = pullback(dot(grads, weight_out, 1, 1))[0].astype(BF)
        return d_pre, dot(d_pre, rows, 0, 0), dot(act.astype(BF), grads, 0, 0), dot(d_pre, weight_in)

    _, far_in, far_out, far_back = expert(far)
    _, near_in, near_out, near_back = expert(near)
    grad_in, grad_out = (near_in + far_in).astype(BF), (near_out + far_out).astype(BF)

    back = (near_back + other_core(far_back.astype(BF)).astype(F32)).astype(BF)
    back = collect(back, "x").astype(BF)
    back = collect(back, "z").astype(BF)
    returned = lax.all_gather(back, "y", axis=0, tiled=True)

    grad_states, grad_queries, keep, send = attention_backward(
        core.reshape(1).astype(jnp.int32),
        place_back,
        returned,
        upstream,
        queries,
        all_keys,
        all_values,
    )

    memory = (keep.astype(F32) + other_core(send).astype(F32)).astype(BF)
    own_rows = mem_keys.shape[0]
    memory = collect(memory, ("y", "x")).astype(BF)
    memory = collect(memory, "z").astype(BF)
    memory = spread(spread(memory, "z"), "x")
    across = other_core(memory)
    grad_keys = jnp.where(core == 0, memory, across)
    grad_values = jnp.where(core == 0, across, memory)
    return grad_states, grad_queries, grad_keys, grad_values, grad_in[None], grad_out[None]


def solution(mesh):
    chips = Mesh(mesh.devices.reshape(4, 16, 4, 2), DEVICES)
    rows, memory, weights = P(DEVICES, None), P("y", None), P("y", PLANE, None)
    return jax.shard_map(
        per_device,
        mesh=chips,
        in_specs=(rows, rows, memory, memory, P(DEVICES), rows, weights, weights, rows),
        out_specs=(rows, rows, memory, memory, weights, weights),
        check_vma=False,
    )
```

```python
import jax
import jax.numpy as jnp
from jax import lax
from jax.experimental import pallas as pl
from jax.experimental.pallas import tpu as pltpu
from jax.sharding import Mesh, PartitionSpec as P

HEAD = 64
GCAP = 2
SCALE = HEAD ** (-0.5)
BF, F32 = jnp.bfloat16, jnp.float32
DEVICES = ("y", "z", "x", "c")
PLANE = ("z", "x", "c")


def dot(left, right, left_dim=1, right_dim=0):
    return lax.dot_general(
        left, right, (((left_dim,), (right_dim,)), ((), ())), preferred_element_type=F32
    )


def exchange(values, axes):
    return lax.all_to_all(values, axes, split_axis=0, concat_axis=0, tiled=True)


def spread(values, axes):
    n = lax.axis_size(axes)
    copies = jnp.broadcast_to(values[None], (n,) + values.shape).reshape(
        (n * values.shape[0],) + values.shape[1:]
    )
    return exchange(copies, axes)


def collect(values, axes):
    n = lax.axis_size(axes)
    got = exchange(values, axes)
    return jnp.sum(got.reshape((n, -1) + got.shape[1:]).astype(F32), axis=0)


def head_pairs(values):
    rows, width = values.shape
    return values.reshape(rows, width // (2 * HEAD), 2 * HEAD).transpose(1, 0, 2)


def rows_of(pairs):
    return pairs.transpose(1, 0, 2).reshape(pairs.shape[1], -1)


def after(values, *others):
    return lax.optimization_barrier((values,) + others)[0]


def shifts(pick):
    n = lax.axis_size("y")
    moves = [[(i, (i + d) % n) for i in range(n)] for d in range(n)]
    return [pick(0)] + [lax.ppermute(pick(d), "y", moves[d]) for d in range(1, n)]


def other_core(values):
    return lax.ppermute(values, "c", [(0, 1), (1, 0)])


def both_heads(block):
    low = lax.broadcasted_iota(jnp.int32, block.shape, 1) < HEAD
    none = jnp.zeros_like(block)
    return jnp.concatenate([jnp.where(low, block, none), jnp.where(low, none, block)], axis=0)


def pair_backward(first, queries, grads, own, across):
    tokens = queries.shape[0]
    keys, values = jnp.where(first, own, across), jnp.where(first, across, own)
    queries, grads = both_heads(queries * BF(SCALE)), both_heads(grads)
    scores = dot(keys, queries, 1, 1)
    exps = jnp.exp(scores - jnp.max(scores, axis=0, keepdims=True))
    probs = exps * (1.0 / jnp.sum(exps, axis=0, keepdims=True))
    d_probs = dot(values, grads, 1, 1)
    centre = jnp.sum(probs * d_probs, axis=0, keepdims=True)
    d_scores = (probs * (d_probs - centre)).astype(BF)
    g_keys = dot(d_scores, queries)
    g_values = dot(probs.astype(BF), grads)
    g_queries = dot(keys, d_scores, 0, 0)
    g_queries = jnp.concatenate([g_queries[:HEAD, :tokens], g_queries[HEAD:, tokens:]], axis=0)
    keep = jnp.where(first, g_keys, g_values).astype(BF)
    send = jnp.where(first, g_values, g_keys).astype(BF)
    return (g_queries.T * SCALE).astype(BF), keep, send


def bulk_kernel(core_ref, free_ref, up_ref, q_ref, own_ref, across_ref, gq_ref, keep_ref, send_ref):
    first = core_ref[0] == 0
    free = free_ref[...]
    for pair in range(q_ref.shape[1] // (2 * HEAD)):
        cols = slice(pair * 2 * HEAD, (pair + 1) * 2 * HEAD)
        gq_ref[:, cols], keep_ref[:, cols], send_ref[:, cols] = pair_backward(
            first, q_ref[:, cols], up_ref[:, cols] * free, own_ref[:, cols], across_ref[:, cols]
        )


def bulk_backward(core, free, upstream, queries, own, across):
    tokens, width = queries.shape
    mem = own.shape[0]
    block = 512
    column = lambda n: pl.BlockSpec((n, block), lambda i: (0, i))
    return pl.pallas_call(
        bulk_kernel,
        grid=(width // block,),
        in_specs=[
            pl.BlockSpec(memory_space=pltpu.SMEM),
            pl.BlockSpec(free.shape, lambda i: (0, 0)),
            column(tokens),
            column(tokens),
            column(mem),
            column(mem),
        ],
        out_specs=[column(tokens), column(mem), column(mem)],
        out_shape=[
            jax.ShapeDtypeStruct((tokens, width), BF),
            jax.ShapeDtypeStruct((mem, width), BF),
            jax.ShapeDtypeStruct((mem, width), BF),
        ],
        cost_estimate=pl.CostEstimate(
            flops=48 * tokens * mem * width, bytes_accessed=32 * mem * width, transcendentals=0
        ),
    )(core, free, upstream, queries, own, across)


def routed_kernel(
    spot_ref, sums_ref, up_ref, q_ref, own_ref, across_ref, ret_ref, keep_ref, send_ref, bulk_ref
):
    first = spot_ref[0] == 0
    tokens = q_ref.shape[0]
    sums = jnp.sum(sums_ref[...].astype(F32), axis=0)
    moe = sums[:tokens].astype(BF)
    bulk_ref[...] = sums[tokens:]
    grads = (up_ref[...].astype(F32) + moe.astype(F32)).astype(BF)
    g_queries, keep_ref[...], send_ref[...] = pair_backward(
        first, q_ref[...], grads, own_ref[...], across_ref[...]
    )
    ret_ref[:, : 2 * HEAD] = moe
    ret_ref[:, 2 * HEAD :] = g_queries


def routed_backward(spot, sums, gathered, queries, own, across):
    tokens, lanes = queries.shape
    mem, more = own.shape[0], sums.shape[1] - tokens
    skip = gathered.shape[1] // lanes // 2
    whole = lambda shape: pl.BlockSpec(shape, lambda i, spot: (0,) * len(shape))
    column = lambda n, base: pl.BlockSpec((n, lanes), lambda i, spot: (0, base + spot[1]))
    outs = [(tokens, 2 * lanes), (mem, lanes), (mem, lanes), (more, lanes)]
    return pl.pallas_call(
        routed_kernel,
        grid_spec=pltpu.PrefetchScalarGridSpec(
            num_scalar_prefetch=1,
            grid=(1,),
            in_specs=[
                whole(sums.shape),
                column(tokens, skip),
                whole(queries.shape),
                column(mem, 0),
                column(mem, 0),
            ],
            out_specs=[whole(shape) for shape in outs],
        ),
        out_shape=[
            jax.ShapeDtypeStruct(shape, dtype) for shape, dtype in zip(outs, (BF, BF, BF, F32))
        ],
    )(spot, sums, gathered, queries, own, across)


def per_device(
    states, queries, mem_keys, mem_values, expert_ids, send_counts, w_in, w_out, upstream
):
    tokens, width = states.shape
    heads = width // HEAD
    window = lax.axis_size("y")
    slots = window * GCAP
    mine, core, depth = lax.axis_index("y"), lax.axis_index("c"), lax.axis_index("z")
    first = core == 0
    own_memory = lax.all_gather(jnp.where(first, mem_keys, mem_values), "y", axis=0, tiled=True)
    across_memory = other_core(own_memory)

    experts = jnp.arange(window, dtype=jnp.int32)
    onehot = (expert_ids[:, None] == experts[None, :]).astype(jnp.int32)
    rank = jnp.sum((jnp.cumsum(onehot, axis=0) - 1) * onehot, axis=1)
    limit = jnp.sum(onehot * send_counts, axis=1)
    slot = jnp.where(rank < limit, expert_ids * GCAP + rank, -1)
    slot_ids = jnp.arange(slots, dtype=jnp.int32)
    place = (slot_ids[:, None] == slot[None, :]).astype(BF)
    payload = [dot(place, part).astype(BF) for part in (queries, states, upstream)]
    flags = jnp.broadcast_to(jnp.repeat(send_counts[0], GCAP).astype(BF)[:, None], (slots, 128))
    group = spread(jnp.concatenate(payload + [flags], axis=1), "y")

    counts = group[:, 3 * width].reshape(window, slots)[:, ::GCAP].astype(jnp.int32)
    offsets = jnp.cumsum(counts, axis=0).astype(jnp.int32) - counts
    order = jnp.arange(GCAP, dtype=jnp.int32)
    position = offsets[:, :, None] + order
    kept = (order < counts[:, :, None]) & (position < GCAP)
    target = jnp.where(kept, experts[None, :, None] * GCAP + position, -1).reshape(-1)
    pack = (slot_ids[:, None] == target[None, :]).astype(BF)
    filled = jnp.sum(pack.astype(F32), axis=1)
    routed = dot(pack, group[:, : 3 * width]).astype(BF)
    own_target = lax.dynamic_slice_in_dim(target, mine * slots, slots, 0)
    steps_back = (mine - slot_ids // GCAP + window) % window * GCAP + slot_ids % GCAP
    own = (own_target[:, None] == steps_back[None, :]).astype(BF)
    place_back = dot(place, own, 0, 0)
    taken = jnp.sum(place_back, axis=1, keepdims=True)
    place_back = place_back.astype(BF)

    in_head = jnp.arange(heads)[:, None] == (jnp.arange(width) // HEAD)[None, :]
    by_head = jnp.where(in_head[:, None, :], routed[None, :, :width], 0).reshape(-1, width)
    scores = dot(by_head, mem_keys, 1, 1) * SCALE
    top = jnp.max(scores, axis=1, keepdims=True)
    exps = jnp.exp(scores - top)
    total = jnp.sum(exps, axis=1)
    part = dot(exps.astype(BF), mem_values).reshape(heads, slots, width)
    part = jnp.sum(jnp.where(in_head[:, None, :], part, 0.0), axis=0)
    tops, totals = top.reshape(heads, slots).T, total.reshape(heads, slots).T
    pad = jnp.zeros((slots, 128 - 2 * heads), F32)
    parts = exchange(jnp.concatenate([part, tops, totals, pad], axis=1), "y")
    parts = parts.reshape(window, GCAP, -1)
    tops, totals = parts[:, :, width : width + heads], parts[:, :, width + heads : width + 2 * heads]
    share = jnp.exp(tops - jnp.max(tops, axis=0))
    share = share / jnp.sum(share * totals, axis=0)
    share = jnp.dot(
        share.reshape(-1, heads), in_head.astype(F32), precision=lax.Precision.HIGHEST
    ).reshape(window, GCAP, width)
    attended = jnp.sum(parts[:, :, :width] * share, axis=0)
    here = lax.dynamic_slice_in_dim(routed, mine * GCAP, GCAP, 0)
    here_filled = lax.dynamic_slice_in_dim(filled, mine * GCAP, GCAP, 0)
    row = (here[:, width : 2 * width].astype(F32) + attended) * here_filled[:, None]
    pair = jnp.concatenate([row.astype(BF), here[:, 2 * width :]], axis=1)

    copies = jnp.broadcast_to(pair[None], (lax.axis_size("z"),) + pair.shape)
    level = exchange(jnp.concatenate([copies, head_pairs(here[:, :width])], axis=2), "z")
    level = level.reshape(-1, level.shape[2])
    routed_queries = level[:, 2 * width :]
    level = level[:, : 2 * width]

    bulk_queries, keep, send = bulk_backward(
        core.reshape(1).astype(jnp.int32),
        (1.0 - taken).astype(BF),
        upstream,
        queries,
        own_memory,
        across_memory,
    )
    near = spread(after(level, send), "x")
    bulk = (keep.astype(F32) + other_core(send).astype(F32)).astype(BF)
    far = other_core(after(near, bulk))
    own_rows = mem_keys.shape[0]
    ahead = lambda d: lax.dynamic_slice_in_dim(bulk, (mine + d) % window * own_rows, own_rows, 0)
    bulk = sum(part.astype(F32) for part in shifts(ahead)).astype(BF)
    weight_in, weight_out = w_in[0], w_out[0]

    def expert(block):
        rows, grads = block[:, :width], block[:, width:]
        pre = dot(rows, weight_in, 1, 1)
        act, pullback = jax.vjp(jax.nn.gelu, pre)
        d_pre = pullback(dot(grads, weight_out, 1, 1))[0].astype(BF)
        return d_pre, dot(d_pre, rows, 0, 0), dot(act.astype(BF), grads, 0, 0), dot(d_pre, weight_in)

    _, far_in, far_out, far_back = expert(far)
    _, near_in, near_out, near_back = expert(near)
    grad_in, grad_out = (near_in + far_in).astype(BF), (near_out + far_out).astype(BF)

    back = (near_back + other_core(far_back.astype(BF)).astype(F32)).astype(BF)
    parts_of_x = lax.axis_size("x")
    joined = jnp.concatenate(
        [back.reshape(parts_of_x, -1, width), bulk.reshape(parts_of_x, -1, width)], axis=1
    )
    joined = collect(joined.reshape(-1, width), "x").astype(BF)
    joined = exchange(head_pairs(joined), "z")
    returned, keep, send, bulk = routed_backward(
        jnp.stack([core, depth]).astype(jnp.int32),
        joined,
        level,
        routed_queries,
        own_memory,
        across_memory,
    )

    memory = (keep.astype(F32) + other_core(send).astype(F32)).astype(BF)
    memory = (collect(memory, ("y", "x")) + bulk).astype(BF)
    copies = jnp.broadcast_to(memory[None], (lax.axis_size("z"),) + memory.shape)
    returned = returned.reshape(copies.shape[0], 2 * GCAP, 2 * HEAD)
    joined = exchange(jnp.concatenate([copies, returned], axis=1), "z")
    memory, returned = joined[:, : memory.shape[0]], joined[:, memory.shape[0] :]
    returned = rows_of(returned).reshape(GCAP, 2 * width)
    returned = jnp.concatenate(shifts(lambda d: returned), axis=0)
    memory = spread(rows_of(memory), ("x", "c")).reshape(parts_of_x, 2, -1, width)
    grad_keys = memory[:, 0].reshape(own_rows, width)
    grad_values = memory[:, 1].reshape(own_rows, width)
    moe_grad = dot(place_back, returned[:, :width])
    grad_states = (upstream.astype(F32) + moe_grad).astype(BF)
    grad_queries = jnp.where(taken > 0, dot(place_back, returned[:, width:]).astype(BF), bulk_queries)
    return grad_states, grad_queries, grad_keys, grad_values, grad_in[None], grad_out[None]


def solution(mesh):
    chips = Mesh(mesh.devices.reshape(4, 16, 4, 2), DEVICES)
    rows, memory, weights = P(DEVICES, None), P("y", None), P("y", PLANE, None)
    return jax.shard_map(
        per_device,
        mesh=chips,
        in_specs=(rows, rows, memory, memory, P(DEVICES), rows, weights, weights, rows),
        out_specs=(rows, rows, memory, memory, weights, weights),
        check_vma=False,
    )
```

```python
import jax
import jax.numpy as jnp
from jax import lax
from jax.experimental import pallas as pl
from jax.experimental.pallas import tpu as pltpu
from jax.sharding import Mesh, PartitionSpec as P

HEAD = 64
GCAP = 2
SCALE = HEAD ** (-0.5)
BF, F32 = jnp.bfloat16, jnp.float32
DEVICES = ("y", "z", "x", "c")
PLANE = ("z", "x", "c")


def dot(left, right, left_dim=1, right_dim=0):
    return lax.dot_general(
        left, right, (((left_dim,), (right_dim,)), ((), ())), preferred_element_type=F32
    )


def exchange(values, axes):
    return lax.all_to_all(values, axes, split_axis=0, concat_axis=0, tiled=True)


def spread(values, axes):
    n = lax.axis_size(axes)
    copies = jnp.broadcast_to(values[None], (n,) + values.shape).reshape(
        (n * values.shape[0],) + values.shape[1:]
    )
    return exchange(copies, axes)


def collect(values, axes):
    n = lax.axis_size(axes)
    got = exchange(values, axes)
    return jnp.sum(got.reshape((n, -1) + got.shape[1:]).astype(F32), axis=0)


def head_pairs(values):
    rows, width = values.shape
    return values.reshape(rows, width // (2 * HEAD), 2 * HEAD).transpose(1, 0, 2)


def rows_of(pairs):
    return pairs.transpose(1, 0, 2).reshape(pairs.shape[1], -1)


def after(values, *others):
    return lax.optimization_barrier((values,) + others)[0]


def shifts(pick):
    n = lax.axis_size("y")
    moves = [[(i, (i + d) % n) for i in range(n)] for d in range(n)]
    return [pick(0)] + [lax.ppermute(pick(d), "y", moves[d]) for d in range(1, n)]


def other_core(values):
    return lax.ppermute(values, "c", [(0, 1), (1, 0)])


def both_heads(block):
    low = lax.broadcasted_iota(jnp.int32, block.shape, 1) < HEAD
    none = jnp.zeros_like(block)
    return jnp.concatenate([jnp.where(low, block, none), jnp.where(low, none, block)], axis=0)


def pair_backward(first, queries, grads, own, across):
    tokens = queries.shape[0]
    keys, values = jnp.where(first, own, across), jnp.where(first, across, own)
    queries, grads = both_heads(queries * BF(SCALE)), both_heads(grads)
    scores = dot(keys, queries, 1, 1)
    exps = jnp.exp(scores - jnp.max(scores, axis=0, keepdims=True))
    probs = exps * (1.0 / jnp.sum(exps, axis=0, keepdims=True))
    d_probs = dot(values, grads, 1, 1)
    centre = jnp.sum(probs * d_probs, axis=0, keepdims=True)
    d_scores = (probs * (d_probs - centre)).astype(BF)
    g_keys = dot(d_scores, queries)
    g_values = dot(probs.astype(BF), grads)
    g_queries = dot(keys, d_scores, 0, 0)
    g_queries = jnp.concatenate([g_queries[:HEAD, :tokens], g_queries[HEAD:, tokens:]], axis=0)
    keep = jnp.where(first, g_keys, g_values).astype(BF)
    send = jnp.where(first, g_values, g_keys).astype(BF)
    return (g_queries.T * SCALE).astype(BF), keep, send


def bulk_kernel(core_ref, free_ref, up_ref, q_ref, own_ref, across_ref, gq_ref, keep_ref, send_ref):
    first = core_ref[0] == 0
    free = free_ref[...]
    for pair in range(q_ref.shape[1] // (2 * HEAD)):
        cols = slice(pair * 2 * HEAD, (pair + 1) * 2 * HEAD)
        gq_ref[:, cols], keep_ref[:, cols], send_ref[:, cols] = pair_backward(
            first, q_ref[:, cols], up_ref[:, cols] * free, own_ref[:, cols], across_ref[:, cols]
        )


def bulk_backward(core, free, upstream, queries, own, across):
    tokens, width = queries.shape
    mem = own.shape[0]
    block = 512
    column = lambda n: pl.BlockSpec((n, block), lambda i: (0, i))
    return pl.pallas_call(
        bulk_kernel,
        grid=(width // block,),
        in_specs=[
            pl.BlockSpec(memory_space=pltpu.SMEM),
            pl.BlockSpec(free.shape, lambda i: (0, 0)),
            column(tokens),
            column(tokens),
            column(mem),
            column(mem),
        ],
        out_specs=[column(tokens), column(mem), column(mem)],
        out_shape=[
            jax.ShapeDtypeStruct((tokens, width), BF),
            jax.ShapeDtypeStruct((mem, width), BF),
            jax.ShapeDtypeStruct((mem, width), BF),
        ],
        cost_estimate=pl.CostEstimate(
            flops=12 * tokens * mem * width, bytes_accessed=8 * mem * width, transcendentals=0
        ),
    )(core, free, upstream, queries, own, across)


def routed_kernel(
    spot_ref, sums_ref, up_ref, q_ref, own_ref, across_ref, ret_ref, keep_ref, send_ref, bulk_ref
):
    first = spot_ref[0] == 0
    tokens = q_ref.shape[0]
    sums = jnp.sum(sums_ref[...].astype(F32), axis=0)
    moe = sums[:tokens].astype(BF)
    bulk_ref[...] = sums[tokens:]
    grads = (up_ref[...].astype(F32) + moe.astype(F32)).astype(BF)
    g_queries, keep_ref[...], send_ref[...] = pair_backward(
        first, q_ref[...], grads, own_ref[...], across_ref[...]
    )
    ret_ref[:tokens] = moe
    ret_ref[tokens:] = g_queries


def routed_backward(spot, sums, gathered, queries, own, across):
    tokens, lanes = queries.shape
    mem, more = own.shape[0], sums.shape[1] - tokens
    whole = lambda shape: pl.BlockSpec(shape, lambda i, spot: (0,) * len(shape))
    column = lambda n: pl.BlockSpec((n, lanes), lambda i, spot: (0, spot[1]))
    outs = [(2 * tokens, lanes), (mem, lanes), (mem, lanes), (more, lanes)]
    return pl.pallas_call(
        routed_kernel,
        grid_spec=pltpu.PrefetchScalarGridSpec(
            num_scalar_prefetch=1,
            grid=(1,),
            in_specs=[
                whole(sums.shape),
                column(tokens),
                whole(queries.shape),
                column(mem),
                column(mem),
            ],
            out_specs=[whole(shape) for shape in outs],
        ),
        out_shape=[
            jax.ShapeDtypeStruct(shape, dtype) for shape, dtype in zip(outs, (BF, BF, BF, F32))
        ],
    )(spot, sums, gathered, queries, own, across)


def pick_kernel(counts_ref, ids_ref, *refs):
    parts, (rows_ref, place_ref) = refs[:-2], refs[-2:]
    slots, tokens = place_ref.shape
    slot = lax.broadcasted_iota(jnp.int32, (slots, tokens), 0)
    expert, order = slot // GCAP, slot % GCAP
    count = jnp.zeros((slots, tokens), jnp.int32)
    for e in range(slots // GCAP):
        count = jnp.where(expert == e, counts_ref[0, e], count)
    named = ids_ref[...] == expert
    earlier = lax.broadcasted_iota(jnp.int32, (tokens, tokens), 0)
    earlier = (earlier < lax.broadcasted_iota(jnp.int32, (tokens, tokens), 1)).astype(BF)
    rank = dot(named.astype(BF), earlier).astype(jnp.int32)
    place = (named & (rank == order) & (rank < count)).astype(BF)
    place_ref[...] = place
    width = parts[0].shape[1]
    for i, part in enumerate(parts):
        rows_ref[:, i * width : (i + 1) * width] = dot(place, part[...]).astype(BF)
    rows_ref[:, len(parts) * width :] = count.astype(F32).astype(BF)


def pick_rows(counts, ids, parts, slots):
    tokens, width = parts[0].shape
    vmem = pl.BlockSpec(memory_space=pltpu.VMEM)
    return pl.pallas_call(
        pick_kernel,
        in_specs=[pl.BlockSpec(memory_space=pltpu.SMEM)] + [vmem] * (1 + len(parts)),
        out_specs=[vmem, vmem],
        out_shape=[
            jax.ShapeDtypeStruct((slots, len(parts) * width + tokens), BF),
            jax.ShapeDtypeStruct((slots, tokens), BF),
        ],
    )(counts, ids, *parts)


def per_device(
    states, queries, mem_keys, mem_values, expert_ids, send_counts, w_in, w_out, upstream
):
    tokens, width = states.shape
    heads = width // HEAD
    window = lax.axis_size("y")
    slots = window * GCAP
    mine, core, depth = lax.axis_index("y"), lax.axis_index("c"), lax.axis_index("z")
    first = core == 0
    own_memory = lax.all_gather(jnp.where(first, mem_keys, mem_values), "y", axis=0, tiled=True)

    experts = jnp.arange(window, dtype=jnp.int32)
    slot_ids = jnp.arange(slots, dtype=jnp.int32)
    picked, place = pick_rows(
        send_counts, expert_ids.reshape(1, tokens), (queries, states, upstream), slots
    )
    group = spread(picked, "y")

    counts = group[:, 3 * width].reshape(window, slots)[:, ::GCAP].astype(jnp.int32)
    offsets = jnp.cumsum(counts, axis=0).astype(jnp.int32) - counts
    order = jnp.arange(GCAP, dtype=jnp.int32)
    position = offsets[:, :, None] + order
    kept = (order < counts[:, :, None]) & (position < GCAP)
    target = jnp.where(kept, experts[None, :, None] * GCAP + position, -1).reshape(-1)
    pack = (slot_ids[:, None] == target[None, :]).astype(BF)
    filled = jnp.sum(pack.astype(F32), axis=1)
    routed = dot(pack, group[:, : 3 * width]).astype(BF)
    own_target = lax.dynamic_slice_in_dim(target, mine * slots, slots, 0)
    own = (own_target[:, None] == slot_ids[None, :]).astype(BF)
    place_back = dot(place, own, 0, 0)
    taken = jnp.sum(place_back, axis=1, keepdims=True)
    place_back = place_back.astype(BF)

    here = lax.dynamic_slice_in_dim(routed, mine * GCAP, GCAP, 0)
    depths = lax.axis_size("z")
    copies = jnp.broadcast_to(here[None, :, 2 * width :], (depths, GCAP, width))
    level = exchange(jnp.concatenate([copies, head_pairs(here[:, :width])], axis=2), "z")
    level = level.reshape(-1, level.shape[2])
    level_grads, routed_queries = level[:, :width], level[:, width:]

    in_head = jnp.arange(heads)[:, None] == (jnp.arange(width) // HEAD)[None, :]
    by_head = jnp.where(in_head[:, None, :], routed[None, :, :width], 0).reshape(-1, width)
    scores = dot(by_head, mem_keys, 1, 1) * SCALE
    top = jnp.max(scores, axis=1, keepdims=True)
    exps = jnp.exp(scores - top)
    total = jnp.sum(exps, axis=1)
    part = dot(exps.astype(BF), mem_values).reshape(heads, slots, width)
    part = jnp.sum(jnp.where(in_head[:, None, :], part, 0.0), axis=0)
    tops, totals = top.reshape(heads, slots).T, total.reshape(heads, slots).T
    pad = jnp.zeros((slots, 128 - 2 * heads), F32)
    parts = exchange(after(jnp.concatenate([part, tops, totals, pad], axis=1), level), "y")
    parts = parts.reshape(window, GCAP, -1)
    tops, totals = parts[:, :, width : width + heads], parts[:, :, width + heads : width + 2 * heads]
    share = jnp.exp(tops - jnp.max(tops, axis=0))
    share = share / jnp.sum(share * totals, axis=0)
    share = jnp.dot(
        share.reshape(-1, heads), in_head.astype(F32), precision=lax.Precision.HIGHEST
    ).reshape(window, GCAP, width)
    attended = jnp.sum(parts[:, :, :width] * share, axis=0)
    here_filled = lax.dynamic_slice_in_dim(filled, mine * GCAP, GCAP, 0)
    row = (here[:, width : 2 * width].astype(F32) + attended) * here_filled[:, None]
    row = row.astype(BF)
    across_memory = other_core(after(own_memory, row))

    level_rows = spread(row, "z")

    bulk_queries, keep, send = bulk_backward(
        core.reshape(1).astype(jnp.int32),
        (1.0 - taken).astype(BF),
        upstream,
        queries,
        own_memory,
        across_memory,
    )
    level = jnp.concatenate([level_rows, level_grads], axis=1)
    near = spread(after(level, send), "x")
    sent = jnp.concatenate([other_core(part) for part in jnp.split(send, 2, axis=0)], axis=0)
    bulk = (keep.astype(F32) + sent.astype(F32)).astype(BF)
    own_rows = mem_keys.shape[0]
    ahead = lambda d: lax.dynamic_slice_in_dim(bulk, (mine + d) % window * own_rows, own_rows, 0)
    bulk = sum(part.astype(F32) for part in shifts(ahead)).astype(BF)
    far = other_core(after(near, bulk))
    weight_in, weight_out = w_in[0], w_out[0]

    def expert(block):
        rows, grads = block[:, :width], block[:, width:]
        pre = dot(rows, weight_in, 1, 1)
        act, pullback = jax.vjp(jax.nn.gelu, pre)
        d_pre = pullback(dot(grads, weight_out, 1, 1))[0].astype(BF)
        return d_pre, dot(d_pre, rows, 0, 0), dot(act.astype(BF), grads, 0, 0), dot(d_pre, weight_in)

    _, far_in, far_out, far_back = expert(far)
    _, near_in, near_out, near_back = expert(near)
    grad_in, grad_out = (near_in + far_in).astype(BF), (near_out + far_out).astype(BF)

    back = (near_back + other_core(far_back.astype(BF)).astype(F32)).astype(BF)
    parts_of_x = lax.axis_size("x")
    joined = jnp.concatenate(
        [back.reshape(parts_of_x, -1, width), bulk.reshape(parts_of_x, -1, width)], axis=1
    )
    joined = collect(joined.reshape(-1, width), "x").astype(BF)
    joined = exchange(head_pairs(joined), "z")
    returned, keep, send, bulk = routed_backward(
        jnp.stack([core, depth]).astype(jnp.int32),
        joined,
        level_grads,
        routed_queries,
        own_memory,
        across_memory,
    )

    memory = (keep.astype(F32) + other_core(send).astype(F32)).astype(BF)
    blocks = window * parts_of_x
    copies = jnp.broadcast_to(returned[None], (blocks,) + returned.shape)
    joined = exchange(
        jnp.concatenate([memory.reshape(blocks, -1, 2 * HEAD), copies], axis=1), ("y", "x")
    )
    rows_of_x = joined.shape[1] - returned.shape[0]
    memory = (jnp.sum(joined[:, :rows_of_x].astype(F32), axis=0) + bulk).astype(BF)
    returned = joined[:, rows_of_x:].reshape((window, parts_of_x) + returned.shape)
    returned = lax.dynamic_index_in_dim(returned, lax.axis_index("x"), 1, False)
    returned = returned.reshape(window, 2, depths, GCAP, 2 * HEAD).transpose(2, 0, 1, 3, 4)
    copies = jnp.broadcast_to(memory[None], (depths,) + memory.shape)
    joined = exchange(
        jnp.concatenate([copies, returned.reshape(depths, -1, 2 * HEAD)], axis=1), "z"
    )
    memory, returned = joined[:, :rows_of_x], rows_of(joined[:, rows_of_x:])
    returned = returned.reshape(window, 2, GCAP, width)
    moe_rows, query_rows = returned[:, 0].reshape(slots, width), returned[:, 1].reshape(slots, width)
    memory = spread(rows_of(memory), ("x", "c")).reshape(parts_of_x, 2, -1, width)
    grad_keys = memory[:, 0].reshape(own_rows, width)
    grad_values = memory[:, 1].reshape(own_rows, width)
    moe_grad = dot(place_back, moe_rows)
    grad_states = (upstream.astype(F32) + moe_grad).astype(BF)
    grad_queries = jnp.where(taken > 0, dot(place_back, query_rows).astype(BF), bulk_queries)
    return grad_states, grad_queries, grad_keys, grad_values, grad_in[None], grad_out[None]


def solution(mesh):
    chips = Mesh(mesh.devices.reshape(4, 16, 4, 2), DEVICES)
    rows, memory, weights = P(DEVICES, None), P("y", None), P("y", PLANE, None)
    return jax.shard_map(
        per_device,
        mesh=chips,
        in_specs=(rows, rows, memory, memory, P(DEVICES), rows, weights, weights, rows),
        out_specs=(rows, rows, memory, memory, weights, weights),
        check_vma=False,
    )
```

```python
import jax
import jax.numpy as jnp
from jax import lax
from jax.experimental import pallas as pl
from jax.experimental.pallas import tpu as pltpu
from jax.sharding import Mesh, PartitionSpec as P

HEAD = 64
GCAP = 2
PIECES = 2
SCALE = HEAD ** (-0.5)
BF, F32 = jnp.bfloat16, jnp.float32
DEVICES = ("y", "z", "x", "c")
PLANE = ("z", "x", "c")


def dot(left, right, left_dim=1, right_dim=0):
    return lax.dot_general(
        left, right, (((left_dim,), (right_dim,)), ((), ())), preferred_element_type=F32
    )


def exchange(values, axes):
    return lax.all_to_all(values, axes, split_axis=0, concat_axis=0, tiled=True)


def spread(values, axes):
    n = lax.axis_size(axes)
    copies = jnp.broadcast_to(values[None], (n,) + values.shape).reshape(
        (n * values.shape[0],) + values.shape[1:]
    )
    return exchange(copies, axes)


def collect(values, axes):
    n = lax.axis_size(axes)
    got = exchange(values, axes)
    return jnp.sum(got.reshape((n, -1) + got.shape[1:]).astype(F32), axis=0)


def head_pairs(values):
    rows, width = values.shape
    return values.reshape(rows, width // (2 * HEAD), 2 * HEAD).transpose(1, 0, 2)


def rows_of(pairs):
    return pairs.transpose(1, 0, 2).reshape(pairs.shape[1], -1)


def after(values, *others):
    return lax.optimization_barrier((values,) + others)[0]


def other_core(values):
    return lax.ppermute(values, "c", [(0, 1), (1, 0)])


def both_heads(block):
    low = lax.broadcasted_iota(jnp.int32, block.shape, 1) < HEAD
    none = jnp.zeros_like(block)
    return jnp.concatenate([jnp.where(low, block, none), jnp.where(low, none, block)], axis=0)


def pair_backward(first, queries, grads, own, across):
    tokens = queries.shape[0]
    keys, values = jnp.where(first, own, across), jnp.where(first, across, own)
    queries, grads = both_heads(queries * BF(SCALE)), both_heads(grads)
    scores = dot(keys, queries, 1, 1)
    exps = jnp.exp(scores - jnp.max(scores, axis=0, keepdims=True))
    probs = exps * (1.0 / jnp.sum(exps, axis=0, keepdims=True))
    d_probs = dot(values, grads, 1, 1)
    centre = jnp.sum(probs * d_probs, axis=0, keepdims=True)
    d_scores = (probs * (d_probs - centre)).astype(BF)
    g_keys = dot(d_scores, queries)
    g_values = dot(probs.astype(BF), grads)
    g_queries = dot(keys, d_scores, 0, 0)
    g_queries = jnp.concatenate([g_queries[:HEAD, :tokens], g_queries[HEAD:, tokens:]], axis=0)
    keep = jnp.where(first, g_keys, g_values).astype(BF)
    send = jnp.where(first, g_values, g_keys).astype(BF)
    return (g_queries.T * SCALE).astype(BF), keep, send


def bulk_kernel(core_ref, free_ref, up_ref, q_ref, own_ref, *refs):
    across, (gq_ref, keep_ref), sends = refs[:PIECES], refs[PIECES : PIECES + 2], refs[PIECES + 2 :]
    first = core_ref[0] == 0
    free = free_ref[...]
    rows = own_ref.shape[0] // PIECES
    for pair in range(q_ref.shape[1] // (2 * HEAD)):
        cols = slice(pair * 2 * HEAD, (pair + 1) * 2 * HEAD)
        gq_ref[:, cols], keep_ref[:, cols], send = pair_backward(
            first,
            q_ref[:, cols],
            up_ref[:, cols] * free,
            own_ref[:, cols],
            jnp.concatenate([ref[:, cols] for ref in across], axis=0),
        )
        for i, ref in enumerate(sends):
            ref[:, cols] = send[i * rows : (i + 1) * rows]


def bulk_backward(core, free, upstream, queries, own, across):
    tokens, width = queries.shape
    mem = own.shape[0]
    block = 512
    column = lambda n: pl.BlockSpec((n, block), lambda i: (0, i))
    outs = [tokens, mem] + [mem // PIECES] * PIECES
    got = pl.pallas_call(
        bulk_kernel,
        grid=(width // block,),
        in_specs=[
            pl.BlockSpec(memory_space=pltpu.SMEM),
            pl.BlockSpec(free.shape, lambda i: (0, 0)),
            column(tokens),
            column(tokens),
            column(mem),
        ]
        + [column(mem // PIECES)] * PIECES,
        out_specs=[column(n) for n in outs],
        out_shape=[jax.ShapeDtypeStruct((n, width), BF) for n in outs],
        cost_estimate=pl.CostEstimate(
            flops=12 * tokens * mem * width, bytes_accessed=8 * mem * width, transcendentals=0
        ),
    )(core, free, upstream, queries, own, *across)
    return got[0], got[1], got[2:]


def routed_kernel(
    spot_ref, sums_ref, up_ref, q_ref, own_ref, across_ref, ret_ref, keep_ref, send_ref, bulk_ref
):
    first = spot_ref[0] == 0
    tokens = q_ref.shape[0]
    sums = jnp.sum(sums_ref[...].astype(F32), axis=0)
    moe = sums[:tokens].astype(BF)
    bulk_ref[...] = sums[tokens:]
    grads = (up_ref[...].astype(F32) + moe.astype(F32)).astype(BF)
    g_queries, keep_ref[...], send_ref[...] = pair_backward(
        first, q_ref[...], grads, own_ref[...], across_ref[...]
    )
    ret_ref[:tokens] = moe
    ret_ref[tokens:] = g_queries


def routed_backward(spot, sums, gathered, queries, own, across):
    tokens, lanes = queries.shape
    mem, more = own.shape[0], sums.shape[1] - tokens
    whole = lambda shape: pl.BlockSpec(shape, lambda i, spot: (0,) * len(shape))
    skip = gathered.shape[1] // lanes // 2
    column = lambda n, base: pl.BlockSpec((n, lanes), lambda i, spot: (0, base + spot[1]))
    outs = [(2 * tokens, lanes), (mem, lanes), (mem, lanes), (more, lanes)]
    return pl.pallas_call(
        routed_kernel,
        grid_spec=pltpu.PrefetchScalarGridSpec(
            num_scalar_prefetch=1,
            grid=(1,),
            in_specs=[
                whole(sums.shape),
                column(tokens, skip),
                whole(queries.shape),
                column(mem, 0),
                column(mem, 0),
            ],
            out_specs=[whole(shape) for shape in outs],
        ),
        out_shape=[
            jax.ShapeDtypeStruct(shape, dtype) for shape, dtype in zip(outs, (BF, BF, BF, F32))
        ],
    )(spot, sums, gathered, queries, own, across)


def pick_kernel(counts_ref, ids_ref, *refs):
    parts, (rows_ref, place_ref) = refs[:-2], refs[-2:]
    slots, tokens = place_ref.shape
    slot = lax.broadcasted_iota(jnp.int32, (slots, tokens), 0)
    expert, order = slot // GCAP, slot % GCAP
    count = jnp.zeros((slots, tokens), jnp.int32)
    for e in range(slots // GCAP):
        count = jnp.where(expert == e, counts_ref[0, e], count)
    named = ids_ref[...] == expert
    earlier = lax.broadcasted_iota(jnp.int32, (tokens, tokens), 0)
    earlier = (earlier < lax.broadcasted_iota(jnp.int32, (tokens, tokens), 1)).astype(BF)
    rank = dot(named.astype(BF), earlier).astype(jnp.int32)
    place = (named & (rank == order) & (rank < count)).astype(BF)
    place_ref[...] = place
    width = parts[0].shape[1]
    for i, part in enumerate(parts):
        rows = dot(place, part[...]).astype(BF)
        for copy in range(rows_ref.shape[0]):
            rows_ref[copy, :, i * width : (i + 1) * width] = rows
    for copy in range(rows_ref.shape[0]):
        rows_ref[copy, :, len(parts) * width :] = count.astype(F32).astype(BF)


def pick_rows(counts, ids, parts, slots, copies):
    tokens, width = parts[0].shape
    vmem = pl.BlockSpec(memory_space=pltpu.VMEM)
    return pl.pallas_call(
        pick_kernel,
        in_specs=[pl.BlockSpec(memory_space=pltpu.SMEM)] + [vmem] * (1 + len(parts)),
        out_specs=[vmem, vmem],
        out_shape=[
            jax.ShapeDtypeStruct((copies, slots, len(parts) * width + tokens), BF),
            jax.ShapeDtypeStruct((slots, tokens), BF),
        ],
    )(counts, ids, *parts)


def per_device(
    states, queries, mem_keys, mem_values, expert_ids, send_counts, w_in, w_out, upstream
):
    tokens, width = states.shape
    heads = width // HEAD
    window = lax.axis_size("y")
    slots = window * GCAP
    mine, core, depth = lax.axis_index("y"), lax.axis_index("c"), lax.axis_index("z")
    first = core == 0
    own_memory = lax.all_gather(jnp.where(first, mem_keys, mem_values), "y", axis=0, tiled=True)

    experts = jnp.arange(window, dtype=jnp.int32)
    slot_ids = jnp.arange(slots, dtype=jnp.int32)
    picked, place = pick_rows(
        send_counts, expert_ids.reshape(1, tokens), (queries, states, upstream), slots, window
    )
    group = exchange(picked, "y").reshape(window * slots, -1)

    counts = group[:, 3 * width].reshape(window, slots)[:, ::GCAP].astype(jnp.int32)
    offsets = jnp.cumsum(counts, axis=0).astype(jnp.int32) - counts
    order = jnp.arange(GCAP, dtype=jnp.int32)
    position = offsets[:, :, None] + order
    kept = (order < counts[:, :, None]) & (position < GCAP)
    target = jnp.where(kept, experts[None, :, None] * GCAP + position, -1).reshape(-1)
    pack = (slot_ids[:, None] == target[None, :]).astype(BF)
    filled = jnp.sum(pack.astype(F32), axis=1)
    routed = dot(pack, group[:, : 3 * width]).astype(BF)
    own_target = lax.dynamic_slice_in_dim(target, mine * slots, slots, 0)
    own = (own_target[:, None] == slot_ids[None, :]).astype(BF)
    place_back = dot(place, own, 0, 0)
    taken = jnp.sum(place_back, axis=1, keepdims=True)
    place_back = place_back.astype(BF)

    in_head = jnp.arange(heads)[:, None] == (jnp.arange(width) // HEAD)[None, :]
    by_head = jnp.where(in_head[:, None, :], routed[None, :, :width], 0).reshape(-1, width)
    scores = dot(by_head, mem_keys, 1, 1) * SCALE
    top = jnp.max(scores, axis=1, keepdims=True)
    exps = jnp.exp(scores - top)
    total = jnp.sum(exps, axis=1)
    part = dot(exps.astype(BF), mem_values).reshape(heads, slots, width)
    part = jnp.sum(jnp.where(in_head[:, None, :], part, 0.0), axis=0)
    tops, totals = top.reshape(heads, slots).T, total.reshape(heads, slots).T
    pad = jnp.zeros((slots, 128 - 2 * heads), F32)
    parts = exchange(jnp.concatenate([part, tops, totals, pad], axis=1), "y")
    parts = parts.reshape(window, GCAP, -1)
    tops, totals = parts[:, :, width : width + heads], parts[:, :, width + heads : width + 2 * heads]
    share = jnp.exp(tops - jnp.max(tops, axis=0))
    share = share / jnp.sum(share * totals, axis=0)
    share = jnp.dot(
        share.reshape(-1, heads), in_head.astype(F32), precision=lax.Precision.HIGHEST
    ).reshape(window, GCAP, width)
    attended = jnp.sum(parts[:, :, :width] * share, axis=0)
    here = lax.dynamic_slice_in_dim(routed, mine * GCAP, GCAP, 0)
    here_filled = lax.dynamic_slice_in_dim(filled, mine * GCAP, GCAP, 0)
    row = (here[:, width : 2 * width].astype(F32) + attended) * here_filled[:, None]
    pair = jnp.concatenate([row.astype(BF), here[:, 2 * width :]], axis=1)

    depths = lax.axis_size("z")
    copies = jnp.broadcast_to(pair[None], (depths,) + pair.shape)
    level = exchange(jnp.concatenate([copies, head_pairs(here[:, :width])], axis=2), "z")
    level = level.reshape(-1, level.shape[2])
    routed_queries = level[:, 2 * width :]
    level = level[:, : 2 * width]
    across_memory = [
        other_core(piece) for piece in jnp.split(after(own_memory, pair), PIECES, axis=0)
    ]

    bulk_queries, keep, send = bulk_backward(
        core.reshape(1).astype(jnp.int32),
        (1.0 - taken).astype(BF),
        upstream,
        queries,
        own_memory,
        across_memory,
    )
    near = spread(after(level, *send), "x")
    sent = jnp.concatenate([other_core(piece) for piece in send], axis=0)
    bulk = (keep.astype(F32) + sent.astype(F32)).astype(BF)
    far = other_core(after(near, bulk))
    weight_in, weight_out = w_in[0], w_out[0]
    parts_of_x = lax.axis_size("x")

    def expert(block):
        rows, grads = block[:, :width], block[:, width:]
        pre = dot(rows, weight_in, 1, 1)
        act, pullback = jax.vjp(jax.nn.gelu, pre)
        d_pre = pullback(dot(grads, weight_out, 1, 1))[0].astype(BF)
        return d_pre, dot(d_pre, rows, 0, 0), dot(act.astype(BF), grads, 0, 0), dot(d_pre, weight_in)

    _, far_in, far_out, far_back = expert(far)
    _, near_in, near_out, near_back = expert(near)
    grad_in, grad_out = (near_in + far_in).astype(BF), (near_out + far_out).astype(BF)

    back = (near_back + other_core(far_back.astype(BF)).astype(F32)).astype(BF)
    half = width // 2
    over_y = lax.psum_scatter(bulk[:, :half], "y", scatter_dimension=0, tiled=True)
    over_x = bulk[:, half:].reshape(window, parts_of_x, -1, half).transpose(1, 0, 2, 3)
    over_x = over_x.reshape(parts_of_x, -1, half)
    over_x = jnp.concatenate(jnp.split(over_x, 2, axis=1), axis=2)
    rows = back.shape[0] // parts_of_x
    back = jnp.concatenate([back.reshape(parts_of_x, rows, width), over_x], axis=1)
    back = collect(back.reshape(-1, width), "x").astype(BF)
    over_x = jnp.concatenate([back[rows:, :half], back[rows:, half:]], axis=0)
    bulk = jnp.concatenate([head_pairs(over_y), head_pairs(over_x)], axis=0)
    joined = exchange(jnp.concatenate([head_pairs(back[:rows]), bulk], axis=1), "z")
    returned, keep, send, bulk = routed_backward(
        jnp.stack([core, depth]).astype(jnp.int32),
        joined,
        level,
        routed_queries,
        own_memory,
        jnp.concatenate(across_memory, axis=0),
    )

    memory = keep.astype(F32) + other_core(send).astype(F32)
    memory = memory.reshape(window, parts_of_x, -1, 2 * HEAD)
    bulk = bulk.reshape(window, -1, 2 * HEAD)
    of_y = (depth < depths // 2) & (experts == mine)
    of_x = (depth >= depths // 2) & (jnp.arange(parts_of_x) == lax.axis_index("x"))
    memory = memory + jnp.where(of_y[:, None, None, None], bulk[None], 0.0)
    memory = (memory + jnp.where(of_x[None, :, None, None], bulk[:, None], 0.0)).astype(BF)
    blocks = window * parts_of_x
    copies = jnp.broadcast_to(returned[None], (blocks,) + returned.shape)
    joined = exchange(
        jnp.concatenate([memory.reshape(blocks, -1, 2 * HEAD), copies], axis=1), ("y", "x")
    )
    rows_of_x = joined.shape[1] - returned.shape[0]
    memory = jnp.sum(joined[:, :rows_of_x].astype(F32), axis=0).astype(BF)
    returned = joined[:, rows_of_x:].reshape((window, parts_of_x) + returned.shape)
    returned = lax.dynamic_index_in_dim(returned, lax.axis_index("x"), 1, False)
    returned = returned.reshape(window, 2, depths, GCAP, 2 * HEAD).transpose(2, 0, 1, 3, 4)
    copies = jnp.broadcast_to(memory[None], (depths,) + memory.shape)
    joined = exchange(
        jnp.concatenate([copies, returned.reshape(depths, -1, 2 * HEAD)], axis=1), "z"
    )
    memory, returned = joined[:, :rows_of_x], rows_of(joined[:, rows_of_x:])
    returned = returned.reshape(window, 2, GCAP, width)
    moe_rows, query_rows = returned[:, 0].reshape(slots, width), returned[:, 1].reshape(slots, width)
    memory = spread(rows_of(memory), ("x", "c")).reshape(parts_of_x, 2, -1, width)
    grad_keys, grad_values = memory[:, 0].reshape(-1, width), memory[:, 1].reshape(-1, width)
    moe_grad = dot(place_back, moe_rows)
    grad_states = (upstream.astype(F32) + moe_grad).astype(BF)
    grad_queries = jnp.where(taken > 0, dot(place_back, query_rows).astype(BF), bulk_queries)
    return grad_states, grad_queries, grad_keys, grad_values, grad_in[None], grad_out[None]


def solution(mesh):
    chips = Mesh(mesh.devices.reshape(4, 16, 4, 2), DEVICES)
    rows, memory, weights = P(DEVICES, None), P("y", None), P("y", PLANE, None)
    return jax.shard_map(
        per_device,
        mesh=chips,
        in_specs=(rows, rows, memory, memory, P(DEVICES), rows, weights, weights, rows),
        out_specs=(rows, rows, memory, memory, weights, weights),
        check_vma=False,
    )
```

```python
import jax
import jax.numpy as jnp
from jax import lax
from jax.experimental import pallas as pl
from jax.experimental.pallas import tpu as pltpu
from jax.sharding import Mesh, PartitionSpec as P

HEAD = 64
GCAP = 2
PIECES = 4
SCALE = HEAD ** (-0.5)
BF, F32 = jnp.bfloat16, jnp.float32
DEVICES = ("y", "z", "x", "c")
PLANE = ("z", "x", "c")


def dot(left, right, left_dim=1, right_dim=0):
    return lax.dot_general(
        left, right, (((left_dim,), (right_dim,)), ((), ())), preferred_element_type=F32
    )


def exchange(values, axes):
    return lax.all_to_all(values, axes, split_axis=0, concat_axis=0, tiled=True)


def spread(values, axes):
    n = lax.axis_size(axes)
    copies = jnp.broadcast_to(values[None], (n,) + values.shape).reshape(
        (n * values.shape[0],) + values.shape[1:]
    )
    return exchange(copies, axes)


def collect(values, axes):
    n = lax.axis_size(axes)
    got = exchange(values, axes)
    return jnp.sum(got.reshape((n, -1) + got.shape[1:]).astype(F32), axis=0)


def join_kernel(spot_ref, keep_ref, got_ref, more_ref, ret_ref, out_ref):
    blocks, rows = out_ref.shape[0], more_ref.shape[0]
    for block in range(blocks):
        part = pl.ds(block * rows, rows)
        memory = keep_ref[part].astype(F32) + got_ref[part].astype(F32)
        memory = memory + jnp.where(spot_ref[0] == block, more_ref[...], 0.0)
        out_ref[block, :rows] = memory.astype(BF)
        out_ref[block, rows:] = ret_ref[...]


def join_blocks(spot, keep, got, more, returned, blocks):
    vmem = pl.BlockSpec(memory_space=pltpu.VMEM)
    shape = (blocks, more.shape[0] + returned.shape[0], more.shape[1])
    return pl.pallas_call(
        join_kernel,
        in_specs=[pl.BlockSpec(memory_space=pltpu.SMEM)] + [vmem] * 4,
        out_specs=vmem,
        out_shape=jax.ShapeDtypeStruct(shape, BF),
    )(spot, keep, got, more, returned)


def head_pairs(values):
    rows, width = values.shape
    return values.reshape(rows, width // (2 * HEAD), 2 * HEAD).transpose(1, 0, 2)


def rows_of(pairs):
    return pairs.transpose(1, 0, 2).reshape(pairs.shape[1], -1)


def after(values, *others):
    return lax.optimization_barrier((values,) + others)[0]


def other_core(values):
    return lax.ppermute(values, "c", [(0, 1), (1, 0)])


def both_heads(block):
    low = lax.broadcasted_iota(jnp.int32, block.shape, 1) < HEAD
    none = jnp.zeros_like(block)
    return jnp.concatenate([jnp.where(low, block, none), jnp.where(low, none, block)], axis=0)


def pair_backward(first, queries, grads, own, across):
    tokens = queries.shape[0]
    keys, values = jnp.where(first, own, across), jnp.where(first, across, own)
    queries, grads = both_heads(queries * BF(SCALE)), both_heads(grads)
    scores = dot(keys, queries, 1, 1)
    exps = jnp.exp(scores - jnp.max(scores, axis=0, keepdims=True))
    probs = exps * (1.0 / jnp.sum(exps, axis=0, keepdims=True))
    d_probs = dot(values, grads, 1, 1)
    centre = jnp.sum(probs * d_probs, axis=0, keepdims=True)
    d_scores = (probs * (d_probs - centre)).astype(BF)
    g_keys = dot(d_scores, queries)
    g_values = dot(probs.astype(BF), grads)
    g_queries = dot(keys, d_scores, 0, 0)
    g_queries = jnp.concatenate([g_queries[:HEAD, :tokens], g_queries[HEAD:, tokens:]], axis=0)
    keep = jnp.where(first, g_keys, g_values).astype(BF)
    send = jnp.where(first, g_values, g_keys).astype(BF)
    return (g_queries.T * SCALE).astype(BF), keep, send


def bulk_kernel(core_ref, free_ref, up_ref, q_ref, own_ref, *refs):
    across, (gq_ref, keep_ref), sends = refs[:PIECES], refs[PIECES : PIECES + 2], refs[PIECES + 2 :]
    first = core_ref[0] == 0
    free = free_ref[...]
    rows = sends[0].shape[0]
    for pair in range(q_ref.shape[1] // (2 * HEAD)):
        cols = slice(pair * 2 * HEAD, (pair + 1) * 2 * HEAD)
        gq_ref[:, cols], keep_ref[:, cols], send = pair_backward(
            first,
            q_ref[:, cols],
            up_ref[:, cols] * free,
            own_ref[:, cols],
            jnp.concatenate([ref[:, cols] for ref in across], axis=0),
        )
        for i, ref in enumerate(sends):
            ref[:, cols] = send[i * rows : (i + 1) * rows]


def bulk_backward(core, free, upstream, queries, own, across):
    tokens, width = queries.shape
    mem = own.shape[0]
    block = 512
    column = lambda n: pl.BlockSpec((n, block), lambda i: (0, i))
    outs = [tokens, mem] + [mem // 2] * 2
    got = pl.pallas_call(
        bulk_kernel,
        grid=(width // block,),
        in_specs=[
            pl.BlockSpec(memory_space=pltpu.SMEM),
            pl.BlockSpec(free.shape, lambda i: (0, 0)),
            column(tokens),
            column(tokens),
            column(mem),
        ]
        + [column(mem // PIECES)] * PIECES,
        out_specs=[column(n) for n in outs],
        out_shape=[jax.ShapeDtypeStruct((n, width), BF) for n in outs],
        cost_estimate=pl.CostEstimate(
            flops=12 * tokens * mem * width, bytes_accessed=8 * mem * width, transcendentals=0
        ),
    )(core, free, upstream, queries, own, *across)
    return got[0], got[1], got[2:]


def routed_kernel(
    spot_ref, sums_ref, up_ref, q_ref, own_ref, across_ref, ret_ref, keep_ref, send_ref, bulk_ref
):
    first = spot_ref[0] == 0
    tokens = q_ref.shape[0]
    sums = jnp.sum(sums_ref[...].astype(F32), axis=0)
    moe = sums[:tokens].astype(BF)
    bulk_ref[...] = sums[tokens:]
    grads = (up_ref[...].astype(F32) + moe.astype(F32)).astype(BF)
    g_queries, keep_ref[...], send_ref[...] = pair_backward(
        first, q_ref[...], grads, own_ref[...], across_ref[...]
    )
    ret_ref[:tokens] = moe
    ret_ref[tokens:] = g_queries


def routed_backward(spot, sums, gathered, queries, own, across):
    tokens, lanes = queries.shape
    mem, more = own.shape[0], sums.shape[1] - tokens
    whole = lambda shape: pl.BlockSpec(shape, lambda i, spot: (0,) * len(shape))
    skip = gathered.shape[1] // lanes // 2
    column = lambda n, base: pl.BlockSpec((n, lanes), lambda i, spot: (0, base + spot[1]))
    outs = [(2 * tokens, lanes), (mem, lanes), (mem, lanes), (more, lanes)]
    return pl.pallas_call(
        routed_kernel,
        grid_spec=pltpu.PrefetchScalarGridSpec(
            num_scalar_prefetch=1,
            grid=(1,),
            in_specs=[
                whole(sums.shape),
                column(tokens, skip),
                whole(queries.shape),
                column(mem, 0),
                column(mem, 0),
            ],
            out_specs=[whole(shape) for shape in outs],
        ),
        out_shape=[
            jax.ShapeDtypeStruct(shape, dtype) for shape, dtype in zip(outs, (BF, BF, BF, F32))
        ],
    )(spot, sums, gathered, queries, own, across)


def pick_kernel(counts_ref, ids_ref, *refs):
    parts, (rows_ref, place_ref) = refs[:-2], refs[-2:]
    slots, tokens = place_ref.shape
    slot = lax.broadcasted_iota(jnp.int32, (slots, tokens), 0)
    expert, order = slot // GCAP, slot % GCAP
    count = jnp.zeros((slots, tokens), jnp.int32)
    for e in range(slots // GCAP):
        count = jnp.where(expert == e, counts_ref[0, e], count)
    named = ids_ref[...] == expert
    earlier = lax.broadcasted_iota(jnp.int32, (tokens, tokens), 0)
    earlier = (earlier < lax.broadcasted_iota(jnp.int32, (tokens, tokens), 1)).astype(BF)
    rank = dot(named.astype(BF), earlier).astype(jnp.int32)
    place = (named & (rank == order) & (rank < count)).astype(BF)
    place_ref[...] = place
    width = parts[0].shape[1]
    for i, part in enumerate(parts):
        rows = dot(place, part[...]).astype(BF)
        for copy in range(rows_ref.shape[0]):
            rows_ref[copy, :, i * width : (i + 1) * width] = rows
    for copy in range(rows_ref.shape[0]):
        rows_ref[copy, :, len(parts) * width :] = count.astype(F32).astype(BF)


def pick_rows(counts, ids, parts, slots, copies):
    tokens, width = parts[0].shape
    vmem = pl.BlockSpec(memory_space=pltpu.VMEM)
    return pl.pallas_call(
        pick_kernel,
        in_specs=[pl.BlockSpec(memory_space=pltpu.SMEM)] + [vmem] * (1 + len(parts)),
        out_specs=[vmem, vmem],
        out_shape=[
            jax.ShapeDtypeStruct((copies, slots, len(parts) * width + tokens), BF),
            jax.ShapeDtypeStruct((slots, tokens), BF),
        ],
    )(counts, ids, *parts)


def per_device(
    states, queries, mem_keys, mem_values, expert_ids, send_counts, w_in, w_out, upstream
):
    tokens, width = states.shape
    heads = width // HEAD
    window = lax.axis_size("y")
    slots = window * GCAP
    mine, core, depth = lax.axis_index("y"), lax.axis_index("c"), lax.axis_index("z")
    first = core == 0
    own_memory = lax.all_gather(jnp.where(first, mem_keys, mem_values), "y", axis=0, tiled=True)

    experts = jnp.arange(window, dtype=jnp.int32)
    slot_ids = jnp.arange(slots, dtype=jnp.int32)
    picked, place = pick_rows(
        send_counts, expert_ids.reshape(1, tokens), (queries, states, upstream), slots, window
    )
    group = exchange(picked, "y").reshape(window * slots, -1)

    counts = group[:, 3 * width].reshape(window, slots)[:, ::GCAP].astype(jnp.int32)
    offsets = jnp.cumsum(counts, axis=0).astype(jnp.int32) - counts
    order = jnp.arange(GCAP, dtype=jnp.int32)
    position = offsets[:, :, None] + order
    kept = (order < counts[:, :, None]) & (position < GCAP)
    target = jnp.where(kept, experts[None, :, None] * GCAP + position, -1).reshape(-1)
    pack = (slot_ids[:, None] == target[None, :]).astype(BF)
    filled = jnp.sum(pack.astype(F32), axis=1)
    routed = dot(pack, group[:, : 3 * width]).astype(BF)
    own_target = lax.dynamic_slice_in_dim(target, mine * slots, slots, 0)
    own = (own_target[:, None] == slot_ids[None, :]).astype(BF)
    place_back = dot(place, own, 0, 0)
    taken = jnp.sum(place_back, axis=1, keepdims=True)
    place_back = place_back.astype(BF)

    in_head = jnp.arange(heads)[:, None] == (jnp.arange(width) // HEAD)[None, :]
    by_head = jnp.where(in_head[:, None, :], routed[None, :, :width], 0).reshape(-1, width)
    scores = dot(by_head, mem_keys, 1, 1) * SCALE
    top = jnp.max(scores, axis=1, keepdims=True)
    exps = jnp.exp(scores - top)
    total = jnp.sum(exps, axis=1)
    part = dot(exps.astype(BF), mem_values).reshape(heads, slots, width)
    part = jnp.sum(jnp.where(in_head[:, None, :], part, 0.0), axis=0)
    tops, totals = top.reshape(heads, slots).T, total.reshape(heads, slots).T
    pad = jnp.zeros((slots, 128 - 2 * heads), F32)
    parts = exchange(jnp.concatenate([part, tops, totals, pad], axis=1), "y")
    parts = parts.reshape(window, GCAP, -1)
    tops, totals = parts[:, :, width : width + heads], parts[:, :, width + heads : width + 2 * heads]
    share = jnp.exp(tops - jnp.max(tops, axis=0))
    share = share / jnp.sum(share * totals, axis=0)
    share = jnp.dot(
        share.reshape(-1, heads), in_head.astype(F32), precision=lax.Precision.HIGHEST
    ).reshape(window, GCAP, width)
    attended = jnp.sum(parts[:, :, :width] * share, axis=0)
    here = lax.dynamic_slice_in_dim(routed, mine * GCAP, GCAP, 0)
    here_filled = lax.dynamic_slice_in_dim(filled, mine * GCAP, GCAP, 0)
    row = (here[:, width : 2 * width].astype(F32) + attended) * here_filled[:, None]
    pair = jnp.concatenate([row.astype(BF), here[:, 2 * width :]], axis=1)

    depths = lax.axis_size("z")
    copies = jnp.broadcast_to(pair[None], (depths,) + pair.shape)
    level = exchange(jnp.concatenate([copies, head_pairs(here[:, :width])], axis=2), "z")
    level = level.reshape(-1, level.shape[2])
    routed_queries = level[:, 2 * width :]
    level = level[:, : 2 * width]
    across_memory = [
        other_core(piece) for piece in jnp.split(after(own_memory, pair), PIECES, axis=0)
    ]

    bulk_queries, keep, send = bulk_backward(
        core.reshape(1).astype(jnp.int32),
        (1.0 - taken).astype(BF),
        upstream,
        queries,
        own_memory,
        across_memory,
    )
    near = spread(after(level, *send), "x")
    sent = jnp.concatenate([other_core(piece) for piece in send], axis=0)
    bulk = (keep.astype(F32) + sent.astype(F32)).astype(BF)
    own_rows = mem_keys.shape[0]
    blocks = [
        lax.dynamic_slice_in_dim(bulk, (mine + d) % window * own_rows, own_rows, 0)
        for d in range(window)
    ]
    moves = [[(i, (i + d) % window) for i in range(window)] for d in range(window)]
    got = [lax.ppermute(blocks[d], "y", moves[d]) for d in (1, 3)]
    far = other_core(after(near, *blocks))
    weight_in, weight_out = w_in[0], w_out[0]
    parts_of_x = lax.axis_size("x")

    def expert(block):
        rows, grads = block[:, :width], block[:, width:]
        pre = dot(rows, weight_in, 1, 1)
        act, pullback = jax.vjp(jax.nn.gelu, pre)
        d_pre = pullback(dot(grads, weight_out, 1, 1))[0].astype(BF)
        return d_pre, dot(d_pre, rows, 0, 0), dot(act.astype(BF), grads, 0, 0), dot(d_pre, weight_in)

    _, far_in, far_out, far_back = expert(far)
    _, near_in, near_out, near_back = expert(near)
    bulk = sum(part.astype(F32) for part in blocks[:1] + [after(part, far_back) for part in got])
    bulk = jnp.stack([bulk.astype(BF), blocks[2]])
    grad_in, grad_out = (near_in + far_in).astype(BF), (near_out + far_out).astype(BF)

    back = (near_back + other_core(far_back.astype(BF)).astype(F32)).astype(BF)
    rows = back.shape[0] // parts_of_x
    back = [back.reshape(parts_of_x, rows, width), bulk.reshape(2, parts_of_x, -1, width).transpose(1, 0, 2, 3).reshape(parts_of_x, -1, width)]
    back = collect(jnp.concatenate(back, axis=1).reshape(-1, width), "x").astype(BF)
    joined = exchange(head_pairs(back), "z")
    returned, keep, send, bulk = routed_backward(
        jnp.stack([core, depth]).astype(jnp.int32),
        joined,
        level,
        routed_queries,
        own_memory,
        jnp.concatenate(across_memory, axis=0),
    )

    blocks = window * parts_of_x
    spot = (mine + 2) % window * parts_of_x + lax.axis_index("x")
    bulk, opposite = jnp.split(bulk, 2, axis=0)
    joined = join_blocks(
        spot.reshape(1).astype(jnp.int32), keep, other_core(send), opposite, returned, blocks
    )
    joined = exchange(joined, ("y", "x"))
    rows_of_x = joined.shape[1] - returned.shape[0]
    memory = (jnp.sum(joined[:, :rows_of_x].astype(F32), axis=0) + bulk).astype(BF)
    returned = joined[:, rows_of_x:].reshape((window, parts_of_x) + returned.shape)
    returned = lax.dynamic_index_in_dim(returned, lax.axis_index("x"), 1, False)
    returned = returned.reshape(window, 2, depths, GCAP, 2 * HEAD).transpose(2, 0, 1, 3, 4)
    copies = jnp.broadcast_to(memory[None], (depths,) + memory.shape)
    joined = exchange(
        jnp.concatenate([copies, returned.reshape(depths, -1, 2 * HEAD)], axis=1), "z"
    )
    memory, returned = joined[:, :rows_of_x], rows_of(joined[:, rows_of_x:])
    returned = returned.reshape(window, 2, GCAP, width)
    moe_rows, query_rows = returned[:, 0].reshape(slots, width), returned[:, 1].reshape(slots, width)
    memory = spread(rows_of(memory), ("x", "c")).reshape(parts_of_x, 2, -1, width)
    grad_keys, grad_values = memory[:, 0].reshape(-1, width), memory[:, 1].reshape(-1, width)
    moe_grad = dot(place_back, moe_rows)
    grad_states = (upstream.astype(F32) + moe_grad).astype(BF)
    grad_queries = jnp.where(taken > 0, dot(place_back, query_rows).astype(BF), bulk_queries)
    return grad_states, grad_queries, grad_keys, grad_values, grad_in[None], grad_out[None]


def solution(mesh):
    chips = Mesh(mesh.devices.reshape(4, 16, 4, 2), DEVICES)
    rows, memory, weights = P(DEVICES, None), P("y", None), P("y", PLANE, None)
    return jax.shard_map(
        per_device,
        mesh=chips,
        in_specs=(rows, rows, memory, memory, P(DEVICES), rows, weights, weights, rows),
        out_specs=(rows, rows, memory, memory, weights, weights),
        check_vma=False,
    )
```

```python
import jax
import jax.numpy as jnp
from jax import lax
from jax.experimental import pallas as pl
from jax.experimental.pallas import tpu as pltpu
from jax.sharding import Mesh, PartitionSpec as P

HEAD = 64
GCAP = 2
PIECES = 2
SCALE = HEAD ** (-0.5)
BF, F32 = jnp.bfloat16, jnp.float32
DEVICES = ("y", "z", "x", "c")
PLANE = ("z", "x", "c")


def dot(left, right, left_dim=1, right_dim=0):
    return lax.dot_general(
        left, right, (((left_dim,), (right_dim,)), ((), ())), preferred_element_type=F32
    )


def exchange(values, axes):
    return lax.all_to_all(values, axes, split_axis=0, concat_axis=0, tiled=True)


def spread(values, axes):
    n = lax.axis_size(axes)
    copies = jnp.broadcast_to(values[None], (n,) + values.shape).reshape(
        (n * values.shape[0],) + values.shape[1:]
    )
    return exchange(copies, axes)


def collect(values, axes):
    n = lax.axis_size(axes)
    got = exchange(values, axes)
    return jnp.sum(got.reshape((n, -1) + got.shape[1:]).astype(F32), axis=0)


def join_kernel(spot_ref, keep_ref, got_ref, more_ref, ret_ref, out_ref):
    blocks, rows = out_ref.shape[0], more_ref.shape[0]
    for block in range(blocks):
        part = pl.ds(block * rows, rows)
        memory = keep_ref[part].astype(F32) + got_ref[part].astype(F32)
        memory = memory + jnp.where(spot_ref[0] == block, more_ref[...], 0.0)
        out_ref[block, :rows] = memory.astype(BF)
        out_ref[block, rows:] = ret_ref[...]


def join_blocks(spot, keep, got, more, returned, blocks):
    vmem = pl.BlockSpec(memory_space=pltpu.VMEM)
    shape = (blocks, more.shape[0] + returned.shape[0], more.shape[1])
    return pl.pallas_call(
        join_kernel,
        in_specs=[pl.BlockSpec(memory_space=pltpu.SMEM)] + [vmem] * 4,
        out_specs=vmem,
        out_shape=jax.ShapeDtypeStruct(shape, BF),
    )(spot, keep, got, more, returned)


def head_pairs(values):
    rows, width = values.shape
    return values.reshape(rows, width // (2 * HEAD), 2 * HEAD).transpose(1, 0, 2)


def rows_of(pairs):
    return pairs.transpose(1, 0, 2).reshape(pairs.shape[1], -1)


def after(values, *others):
    return lax.optimization_barrier((values,) + others)[0]


def other_core(values):
    return lax.ppermute(values, "c", [(0, 1), (1, 0)])


def both_heads(block):
    low = lax.broadcasted_iota(jnp.int32, block.shape, 1) < HEAD
    none = jnp.zeros_like(block)
    return jnp.concatenate([jnp.where(low, block, none), jnp.where(low, none, block)], axis=0)


def pair_backward(first, queries, grads, own, across):
    tokens = queries.shape[0]
    keys, values = jnp.where(first, own, across), jnp.where(first, across, own)
    queries, grads = both_heads(queries * BF(SCALE)), both_heads(grads)
    scores = dot(keys, queries, 1, 1)
    exps = jnp.exp(scores - jnp.max(scores, axis=0, keepdims=True))
    probs = exps * (1.0 / jnp.sum(exps, axis=0, keepdims=True))
    d_probs = dot(values, grads, 1, 1)
    centre = jnp.sum(probs * d_probs, axis=0, keepdims=True)
    d_scores = (probs * (d_probs - centre)).astype(BF)
    g_keys = dot(d_scores, queries)
    g_values = dot(probs.astype(BF), grads)
    g_queries = dot(keys, d_scores, 0, 0)
    g_queries = jnp.concatenate([g_queries[:HEAD, :tokens], g_queries[HEAD:, tokens:]], axis=0)
    keep = jnp.where(first, g_keys, g_values).astype(BF)
    send = jnp.where(first, g_values, g_keys).astype(BF)
    return (g_queries.T * SCALE).astype(BF), keep, send


def bulk_kernel(
    core_ref, free_ref, up_ref, q_ref, own_ref, across_ref, gq_ref, keep_ref, send_ref
):
    first = core_ref[0] == 0
    free = free_ref[...]
    for pair in range(q_ref.shape[1] // (2 * HEAD)):
        cols = slice(pair * 2 * HEAD, (pair + 1) * 2 * HEAD)
        gq_ref[:, cols], keep_ref[:, cols], send_ref[:, cols] = pair_backward(
            first, q_ref[:, cols], up_ref[:, cols] * free, own_ref[:, cols], across_ref[:, cols]
        )


def bulk_backward(core, free, upstream, queries, own, across, piece):
    tokens = queries.shape[0]
    mem, width = across.shape
    block = 512
    skip = piece * (width // block)
    part = lambda n: pl.BlockSpec((n, block), lambda i: (0, skip + i))
    column = lambda n: pl.BlockSpec((n, block), lambda i: (0, i))
    return pl.pallas_call(
        bulk_kernel,
        grid=(width // block,),
        in_specs=[
            pl.BlockSpec(memory_space=pltpu.SMEM),
            pl.BlockSpec(free.shape, lambda i: (0, 0)),
            part(tokens),
            part(tokens),
            part(mem),
            column(mem),
        ],
        out_specs=[column(tokens), column(mem), column(mem)],
        out_shape=[jax.ShapeDtypeStruct((n, width), BF) for n in (tokens, mem, mem)],
        cost_estimate=pl.CostEstimate(
            flops=12 * tokens * mem * width, bytes_accessed=8 * mem * width, transcendentals=0
        ),
    )(core, free, upstream, queries, own, across)


def routed_kernel(
    spot_ref, sums_ref, up_ref, q_ref, own_ref, across_ref, ret_ref, keep_ref, send_ref, bulk_ref
):
    first = spot_ref[0] == 0
    tokens = q_ref.shape[0]
    sums = jnp.sum(sums_ref[...].astype(F32), axis=0)
    moe = sums[:tokens].astype(BF)
    bulk_ref[...] = sums[tokens:]
    grads = (up_ref[...].astype(F32) + moe.astype(F32)).astype(BF)
    g_queries, keep_ref[...], send_ref[...] = pair_backward(
        first, q_ref[...], grads, own_ref[...], across_ref[...]
    )
    ret_ref[:tokens] = moe
    ret_ref[tokens:] = g_queries


def routed_backward(spot, sums, gathered, queries, own, across):
    tokens, lanes = queries.shape
    mem, more = own.shape[0], sums.shape[1] - tokens
    whole = lambda shape: pl.BlockSpec(shape, lambda i, spot: (0,) * len(shape))
    skip = gathered.shape[1] // lanes // 2
    column = lambda n, base: pl.BlockSpec((n, lanes), lambda i, spot: (0, base + spot[1]))
    outs = [(2 * tokens, lanes), (mem, lanes), (mem, lanes), (more, lanes)]
    return pl.pallas_call(
        routed_kernel,
        grid_spec=pltpu.PrefetchScalarGridSpec(
            num_scalar_prefetch=1,
            grid=(1,),
            in_specs=[
                whole(sums.shape),
                column(tokens, skip),
                whole(queries.shape),
                column(mem, 0),
                column(mem, 0),
            ],
            out_specs=[whole(shape) for shape in outs],
        ),
        out_shape=[
            jax.ShapeDtypeStruct(shape, dtype) for shape, dtype in zip(outs, (BF, BF, BF, F32))
        ],
    )(spot, sums, gathered, queries, own, across)


def pick_kernel(counts_ref, ids_ref, *refs):
    parts, (rows_ref, place_ref) = refs[:-2], refs[-2:]
    slots, tokens = place_ref.shape
    slot = lax.broadcasted_iota(jnp.int32, (slots, tokens), 0)
    expert, order = slot // GCAP, slot % GCAP
    count = jnp.zeros((slots, tokens), jnp.int32)
    for e in range(slots // GCAP):
        count = jnp.where(expert == e, counts_ref[0, e], count)
    named = ids_ref[...] == expert
    earlier = lax.broadcasted_iota(jnp.int32, (tokens, tokens), 0)
    earlier = (earlier < lax.broadcasted_iota(jnp.int32, (tokens, tokens), 1)).astype(BF)
    rank = dot(named.astype(BF), earlier).astype(jnp.int32)
    place = (named & (rank == order) & (rank < count)).astype(BF)
    place_ref[...] = place
    width = parts[0].shape[1]
    for i, part in enumerate(parts):
        rows = dot(place, part[...]).astype(BF)
        for copy in range(rows_ref.shape[0]):
            rows_ref[copy, :, i * width : (i + 1) * width] = rows
    for copy in range(rows_ref.shape[0]):
        rows_ref[copy, :, len(parts) * width :] = count.astype(F32).astype(BF)


def pick_rows(counts, ids, parts, slots, copies):
    tokens, width = parts[0].shape
    vmem = pl.BlockSpec(memory_space=pltpu.VMEM)
    return pl.pallas_call(
        pick_kernel,
        in_specs=[pl.BlockSpec(memory_space=pltpu.SMEM)] + [vmem] * (1 + len(parts)),
        out_specs=[vmem, vmem],
        out_shape=[
            jax.ShapeDtypeStruct((copies, slots, len(parts) * width + tokens), BF),
            jax.ShapeDtypeStruct((slots, tokens), BF),
        ],
    )(counts, ids, *parts)


def per_device(
    states, queries, mem_keys, mem_values, expert_ids, send_counts, w_in, w_out, upstream
):
    tokens, width = states.shape
    heads = width // HEAD
    window = lax.axis_size("y")
    slots = window * GCAP
    mine, core, depth = lax.axis_index("y"), lax.axis_index("c"), lax.axis_index("z")
    first = core == 0

    experts = jnp.arange(window, dtype=jnp.int32)
    slot_ids = jnp.arange(slots, dtype=jnp.int32)
    picked, place = pick_rows(
        send_counts, expert_ids.reshape(1, tokens), (queries, states, upstream), slots, window
    )
    own_memory = jnp.where(first, after(mem_keys, picked), mem_values)
    own_memory = lax.all_gather(own_memory, "y", axis=0, tiled=True)
    group = exchange(picked, "y").reshape(window * slots, -1)

    counts = group[:, 3 * width].reshape(window, slots)[:, ::GCAP].astype(jnp.int32)
    offsets = jnp.cumsum(counts, axis=0).astype(jnp.int32) - counts
    order = jnp.arange(GCAP, dtype=jnp.int32)
    position = offsets[:, :, None] + order
    kept = (order < counts[:, :, None]) & (position < GCAP)
    target = jnp.where(kept, experts[None, :, None] * GCAP + position, -1).reshape(-1)
    pack = (slot_ids[:, None] == target[None, :]).astype(BF)
    filled = jnp.sum(pack.astype(F32), axis=1)
    routed = dot(pack, group[:, : 3 * width]).astype(BF)
    own_target = lax.dynamic_slice_in_dim(target, mine * slots, slots, 0)
    own = (own_target[:, None] == slot_ids[None, :]).astype(BF)
    place_back = dot(place, own, 0, 0)
    taken = jnp.sum(place_back, axis=1, keepdims=True)
    place_back = place_back.astype(BF)

    in_head = jnp.arange(heads)[:, None] == (jnp.arange(width) // HEAD)[None, :]
    by_head = jnp.where(in_head[:, None, :], routed[None, :, :width], 0).reshape(-1, width)
    scores = dot(by_head, mem_keys, 1, 1) * SCALE
    top = jnp.max(scores, axis=1, keepdims=True)
    exps = jnp.exp(scores - top)
    total = jnp.sum(exps, axis=1)
    part = dot(exps.astype(BF), mem_values).reshape(heads, slots, width)
    part = jnp.sum(jnp.where(in_head[:, None, :], part, 0.0), axis=0)
    tops, totals = top.reshape(heads, slots).T, total.reshape(heads, slots).T
    pad = jnp.zeros((slots, 128 - 2 * heads), F32)
    parts = exchange(jnp.concatenate([part, tops, totals, pad], axis=1), "y")
    parts = parts.reshape(window, GCAP, -1)
    tops, totals = parts[:, :, width : width + heads], parts[:, :, width + heads : width + 2 * heads]
    share = jnp.exp(tops - jnp.max(tops, axis=0))
    share = share / jnp.sum(share * totals, axis=0)
    share = jnp.dot(
        share.reshape(-1, heads), in_head.astype(F32), precision=lax.Precision.HIGHEST
    ).reshape(window, GCAP, width)
    attended = jnp.sum(parts[:, :, :width] * share, axis=0)
    here = lax.dynamic_slice_in_dim(routed, mine * GCAP, GCAP, 0)
    here_filled = lax.dynamic_slice_in_dim(filled, mine * GCAP, GCAP, 0)
    row = (here[:, width : 2 * width].astype(F32) + attended) * here_filled[:, None]
    pair = jnp.concatenate([row.astype(BF), here[:, 2 * width :]], axis=1)

    depths = lax.axis_size("z")
    copies = jnp.broadcast_to(pair[None], (depths,) + pair.shape)
    level = exchange(jnp.concatenate([copies, head_pairs(here[:, :width])], axis=2), "z")
    level = level.reshape(-1, level.shape[2])
    routed_queries = level[:, 2 * width :]
    level = level[:, : 2 * width]
    across_memory = [
        other_core(piece) for piece in jnp.split(after(own_memory, pair), PIECES, axis=1)
    ]

    bulk = [
        bulk_backward(
            core.reshape(1).astype(jnp.int32),
            (1.0 - taken).astype(BF),
            upstream,
            queries,
            own_memory,
            across_memory[piece],
            piece,
        )
        for piece in range(PIECES)
    ]
    near = spread(after(level, *across_memory), "x")
    bulk_queries = jnp.concatenate([part[0] for part in bulk], axis=1)
    bulk = jnp.concatenate(
        [(keep.astype(F32) + other_core(send).astype(F32)).astype(BF) for _, keep, send in bulk],
        axis=1,
    )
    own_rows = mem_keys.shape[0]
    blocks = [
        lax.dynamic_slice_in_dim(bulk, (mine + d) % window * own_rows, own_rows, 0)
        for d in range(window)
    ]
    moves = [[(i, (i + d) % window) for i in range(window)] for d in range(window)]
    got = [lax.ppermute(blocks[d], "y", moves[d]) for d in (1, 3)]
    far = other_core(near)
    weight_in, weight_out = w_in[0], w_out[0]
    parts_of_x = lax.axis_size("x")

    def expert(block):
        rows, grads = block[:, :width], block[:, width:]
        pre = dot(rows, weight_in, 1, 1)
        act, pullback = jax.vjp(jax.nn.gelu, pre)
        d_pre = pullback(dot(grads, weight_out, 1, 1))[0].astype(BF)
        return d_pre, dot(d_pre, rows, 0, 0), dot(act.astype(BF), grads, 0, 0), dot(d_pre, weight_in)

    _, far_in, far_out, far_back = expert(far)
    _, near_in, near_out, near_back = expert(near)
    bulk = sum(part.astype(F32) for part in blocks[:1] + [after(part, far_back) for part in got])
    bulk = jnp.stack([bulk.astype(BF), blocks[2]])
    grad_in, grad_out = (near_in + far_in).astype(BF), (near_out + far_out).astype(BF)

    back = (near_back + other_core(far_back.astype(BF)).astype(F32)).astype(BF)
    rows = back.shape[0] // parts_of_x
    back = [back.reshape(parts_of_x, rows, width), bulk.reshape(2, parts_of_x, -1, width).transpose(1, 0, 2, 3).reshape(parts_of_x, -1, width)]
    back = collect(jnp.concatenate(back, axis=1).reshape(-1, width), "x").astype(BF)
    joined = exchange(head_pairs(back), "z")
    returned, keep, send, bulk = routed_backward(
        jnp.stack([core, depth]).astype(jnp.int32),
        joined,
        level,
        routed_queries,
        own_memory,
        jnp.concatenate(across_memory, axis=1),
    )

    blocks = window * parts_of_x
    spot = (mine + 2) % window * parts_of_x + lax.axis_index("x")
    bulk, opposite = jnp.split(bulk, 2, axis=0)
    joined = join_blocks(
        spot.reshape(1).astype(jnp.int32), keep, other_core(send), opposite, returned, blocks
    )
    joined = exchange(joined, ("y", "x"))
    rows_of_x = joined.shape[1] - returned.shape[0]
    memory = (jnp.sum(joined[:, :rows_of_x].astype(F32), axis=0) + bulk).astype(BF)
    returned = joined[:, rows_of_x:].reshape((window, parts_of_x) + returned.shape)
    returned = lax.dynamic_index_in_dim(returned, lax.axis_index("x"), 1, False)
    returned = returned.reshape(window, 2, depths, GCAP, 2 * HEAD).transpose(2, 0, 1, 3, 4)
    copies = jnp.broadcast_to(memory[None], (depths,) + memory.shape)
    joined = exchange(
        jnp.concatenate([copies, returned.reshape(depths, -1, 2 * HEAD)], axis=1), "z"
    )
    memory, returned = joined[:, :rows_of_x], rows_of(joined[:, rows_of_x:])
    returned = returned.reshape(window, 2, GCAP, width)
    moe_rows, query_rows = returned[:, 0].reshape(slots, width), returned[:, 1].reshape(slots, width)
    memory = spread(rows_of(memory), ("x", "c")).reshape(parts_of_x, 2, -1, width)
    grad_keys, grad_values = memory[:, 0].reshape(-1, width), memory[:, 1].reshape(-1, width)
    moe_grad = dot(place_back, moe_rows)
    grad_states = (upstream.astype(F32) + moe_grad).astype(BF)
    grad_queries = jnp.where(taken > 0, dot(place_back, query_rows).astype(BF), bulk_queries)
    return grad_states, grad_queries, grad_keys, grad_values, grad_in[None], grad_out[None]


def solution(mesh):
    chips = Mesh(mesh.devices.reshape(4, 16, 4, 2), DEVICES)
    rows, memory, weights = P(DEVICES, None), P("y", None), P("y", PLANE, None)
    return jax.shard_map(
        per_device,
        mesh=chips,
        in_specs=(rows, rows, memory, memory, P(DEVICES), rows, weights, weights, rows),
        out_specs=(rows, rows, memory, memory, weights, weights),
        check_vma=False,
    )
```

```python
import jax
import jax.numpy as jnp
from jax import lax
from jax.experimental import pallas as pl
from jax.experimental.pallas import tpu as pltpu
from jax.sharding import Mesh, PartitionSpec as P

HEAD = 64
GCAP = 2
PIECES = 2
SCALE = HEAD ** (-0.5)
BF, F32 = jnp.bfloat16, jnp.float32
DEVICES = ("y", "z", "x", "c")
PLANE = ("z", "x", "c")


def dot(left, right, left_dim=1, right_dim=0):
    return lax.dot_general(
        left, right, (((left_dim,), (right_dim,)), ((), ())), preferred_element_type=F32
    )


def exchange(values, axes):
    return lax.all_to_all(values, axes, split_axis=0, concat_axis=0, tiled=True)


def spread(values, axes):
    n = lax.axis_size(axes)
    copies = jnp.broadcast_to(values[None], (n,) + values.shape).reshape(
        (n * values.shape[0],) + values.shape[1:]
    )
    return exchange(copies, axes)


def collect(values, axes):
    n = lax.axis_size(axes)
    got = exchange(values, axes)
    return jnp.sum(got.reshape((n, -1) + got.shape[1:]).astype(F32), axis=0)


def join_kernel(keep_ref, got_ref, ret_ref, out_ref):
    blocks = out_ref.shape[0]
    rows = keep_ref.shape[0] // blocks
    for block in range(blocks):
        part = pl.ds(block * rows, rows)
        memory = keep_ref[part].astype(F32) + got_ref[part].astype(F32)
        out_ref[block, :rows] = memory.astype(BF)
        out_ref[block, rows:] = ret_ref[...]


def join_blocks(keep, got, returned, blocks):
    vmem = pl.BlockSpec(memory_space=pltpu.VMEM)
    shape = (blocks, keep.shape[0] // blocks + returned.shape[0], keep.shape[1])
    return pl.pallas_call(
        join_kernel,
        in_specs=[vmem] * 3,
        out_specs=vmem,
        out_shape=jax.ShapeDtypeStruct(shape, BF),
    )(keep, got, returned)


def sum_kernel(parts_ref, out_ref):
    for pair in range(out_ref.shape[0]):
        cols = slice(pair * 2 * HEAD, (pair + 1) * 2 * HEAD)
        total = parts_ref[0, :, cols].astype(F32)
        for part in range(1, parts_ref.shape[0]):
            total = total + parts_ref[part, :, cols].astype(F32)
        out_ref[pair] = total.astype(BF)


def sum_by_pairs(parts):
    vmem = pl.BlockSpec(memory_space=pltpu.VMEM)
    shape = (parts.shape[2] // (2 * HEAD), parts.shape[1], 2 * HEAD)
    return pl.pallas_call(
        sum_kernel, in_specs=[vmem], out_specs=vmem, out_shape=jax.ShapeDtypeStruct(shape, BF)
    )(parts)


def head_pairs(values):
    rows, width = values.shape
    return values.reshape(rows, width // (2 * HEAD), 2 * HEAD).transpose(1, 0, 2)


def rows_of(pairs):
    return pairs.transpose(1, 0, 2).reshape(pairs.shape[1], -1)


def after(values, *others):
    return lax.optimization_barrier((values,) + others)[0]


def other_core(values):
    return lax.ppermute(values, "c", [(0, 1), (1, 0)])


def both_heads(block):
    low = lax.broadcasted_iota(jnp.int32, block.shape, 1) < HEAD
    none = jnp.zeros_like(block)
    return jnp.concatenate([jnp.where(low, block, none), jnp.where(low, none, block)], axis=0)


def pair_backward(first, queries, grads, own, across):
    tokens = queries.shape[0]
    keys, values = jnp.where(first, own, across), jnp.where(first, across, own)
    queries, grads = both_heads(queries * BF(SCALE)), both_heads(grads)
    scores = dot(keys, queries, 1, 1)
    exps = jnp.exp(scores - jnp.max(scores, axis=0, keepdims=True))
    probs = exps * (1.0 / jnp.sum(exps, axis=0, keepdims=True))
    d_probs = dot(values, grads, 1, 1)
    centre = jnp.sum(probs * d_probs, axis=0, keepdims=True)
    d_scores = (probs * (d_probs - centre)).astype(BF)
    g_keys = dot(d_scores, queries)
    g_values = dot(probs.astype(BF), grads)
    g_queries = dot(keys, d_scores, 0, 0)
    g_queries = jnp.concatenate([g_queries[:HEAD, :tokens], g_queries[HEAD:, tokens:]], axis=0)
    keep = jnp.where(first, g_keys, g_values).astype(BF)
    send = jnp.where(first, g_values, g_keys).astype(BF)
    return (g_queries.T * SCALE).astype(BF), keep, send


def bulk_kernel(
    core_ref, free_ref, up_ref, q_ref, own_ref, across_ref, gq_ref, keep_ref, send_ref
):
    first = core_ref[0] == 0
    free = free_ref[...]
    for pair in range(q_ref.shape[1] // (2 * HEAD)):
        cols = slice(pair * 2 * HEAD, (pair + 1) * 2 * HEAD)
        gq_ref[:, cols], keep_ref[:, cols], send_ref[:, cols] = pair_backward(
            first, q_ref[:, cols], up_ref[:, cols] * free, own_ref[:, cols], across_ref[:, cols]
        )


def bulk_backward(core, free, upstream, queries, own, across, piece):
    tokens = queries.shape[0]
    mem, width = across.shape
    block = 512
    skip = piece * (width // block)
    part = lambda n: pl.BlockSpec((n, block), lambda i: (0, skip + i))
    column = lambda n: pl.BlockSpec((n, block), lambda i: (0, i))
    return pl.pallas_call(
        bulk_kernel,
        grid=(width // block,),
        in_specs=[
            pl.BlockSpec(memory_space=pltpu.SMEM),
            pl.BlockSpec(free.shape, lambda i: (0, 0)),
            part(tokens),
            part(tokens),
            part(mem),
            column(mem),
        ],
        out_specs=[column(tokens), column(mem), column(mem)],
        out_shape=[jax.ShapeDtypeStruct((n, width), BF) for n in (tokens, mem, mem)],
        cost_estimate=pl.CostEstimate(
            flops=12 * tokens * mem * width, bytes_accessed=8 * mem * width, transcendentals=0
        ),
    )(core, free, upstream, queries, own, across)


def routed_kernel(
    spot_ref, sums_ref, up_ref, q_ref, own_ref, across_ref, ret_ref, keep_ref, send_ref, bulk_ref
):
    first = spot_ref[0] == 0
    tokens = q_ref.shape[0]
    sums = jnp.sum(sums_ref[...].astype(F32), axis=0)
    moe = sums[:tokens].astype(BF)
    bulk_ref[...] = sums[tokens:]
    grads = (up_ref[...].astype(F32) + moe.astype(F32)).astype(BF)
    g_queries, keep_ref[...], send_ref[...] = pair_backward(
        first, q_ref[...], grads, own_ref[...], across_ref[...]
    )
    ret_ref[:tokens] = moe
    ret_ref[tokens:] = g_queries


def routed_backward(spot, sums, gathered, queries, own, across):
    tokens, lanes = queries.shape
    mem, more = own.shape[0], sums.shape[1] - tokens
    whole = lambda shape: pl.BlockSpec(shape, lambda i, spot: (0,) * len(shape))
    skip = gathered.shape[1] // lanes // 2
    column = lambda n, base: pl.BlockSpec((n, lanes), lambda i, spot: (0, base + spot[1]))
    outs = [(2 * tokens, lanes), (mem, lanes), (mem, lanes), (more, lanes)]
    return pl.pallas_call(
        routed_kernel,
        grid_spec=pltpu.PrefetchScalarGridSpec(
            num_scalar_prefetch=1,
            grid=(1,),
            in_specs=[
                whole(sums.shape),
                column(tokens, skip),
                whole(queries.shape),
                column(mem, 0),
                column(mem, 0),
            ],
            out_specs=[whole(shape) for shape in outs],
        ),
        out_shape=[
            jax.ShapeDtypeStruct(shape, dtype) for shape, dtype in zip(outs, (BF, BF, BF, F32))
        ],
    )(spot, sums, gathered, queries, own, across)


def pick_kernel(core_ref, counts_ref, ids_ref, keys_ref, values_ref, *refs):
    parts, (rows_ref, place_ref, own_ref) = refs[:-3], refs[-3:]
    own_ref[...] = jnp.where(core_ref[0] == 0, keys_ref[...], values_ref[...])
    slots, tokens = place_ref.shape
    slot = lax.broadcasted_iota(jnp.int32, (slots, tokens), 0)
    expert, order = slot // GCAP, slot % GCAP
    count = jnp.zeros((slots, tokens), jnp.int32)
    for e in range(slots // GCAP):
        count = jnp.where(expert == e, counts_ref[0, e], count)
    named = ids_ref[...] == expert
    earlier = lax.broadcasted_iota(jnp.int32, (tokens, tokens), 0)
    earlier = (earlier < lax.broadcasted_iota(jnp.int32, (tokens, tokens), 1)).astype(BF)
    rank = dot(named.astype(BF), earlier).astype(jnp.int32)
    place = (named & (rank == order) & (rank < count)).astype(BF)
    place_ref[...] = place
    width = parts[0].shape[1]
    for i, part in enumerate(parts):
        rows = dot(place, part[...]).astype(BF)
        for copy in range(rows_ref.shape[0]):
            rows_ref[copy, :, i * width : (i + 1) * width] = rows
    for copy in range(rows_ref.shape[0]):
        rows_ref[copy, :, len(parts) * width :] = count.astype(F32).astype(BF)


def pick_rows(core, counts, ids, keys, values, parts, slots, copies):
    tokens, width = parts[0].shape
    vmem = pl.BlockSpec(memory_space=pltpu.VMEM)
    return pl.pallas_call(
        pick_kernel,
        in_specs=[pl.BlockSpec(memory_space=pltpu.SMEM)] * 2 + [vmem] * (3 + len(parts)),
        out_specs=[vmem] * 3,
        out_shape=[
            jax.ShapeDtypeStruct((copies, slots, len(parts) * width + tokens), BF),
            jax.ShapeDtypeStruct((slots, tokens), BF),
            jax.ShapeDtypeStruct(keys.shape, BF),
        ],
    )(core, counts, ids, keys, values, *parts)


def per_device(
    states, queries, mem_keys, mem_values, expert_ids, send_counts, w_in, w_out, upstream
):
    tokens, width = states.shape
    heads = width // HEAD
    window = lax.axis_size("y")
    slots = window * GCAP
    mine, core, depth = lax.axis_index("y"), lax.axis_index("c"), lax.axis_index("z")
    first = core == 0

    experts = jnp.arange(window, dtype=jnp.int32)
    slot_ids = jnp.arange(slots, dtype=jnp.int32)
    core_id = core.reshape(1).astype(jnp.int32)
    picked, place, own_memory = pick_rows(
        core_id,
        send_counts,
        expert_ids.reshape(1, tokens),
        mem_keys,
        mem_values,
        (queries, states, upstream),
        slots,
        window,
    )
    own_memory = lax.all_gather(own_memory, "y", axis=0, tiled=True)
    group = exchange(picked, "y").reshape(window * slots, -1)

    counts = group[:, 3 * width].reshape(window, slots)[:, ::GCAP].astype(jnp.int32)
    offsets = jnp.cumsum(counts, axis=0).astype(jnp.int32) - counts
    order = jnp.arange(GCAP, dtype=jnp.int32)
    position = offsets[:, :, None] + order
    kept = (order < counts[:, :, None]) & (position < GCAP)
    target = jnp.where(kept, experts[None, :, None] * GCAP + position, -1).reshape(-1)
    pack = (slot_ids[:, None] == target[None, :]).astype(BF)
    filled = jnp.sum(pack.astype(F32), axis=1)
    routed = dot(pack, group[:, : 3 * width]).astype(BF)
    own_target = lax.dynamic_slice_in_dim(target, mine * slots, slots, 0)
    own = (own_target[:, None] == slot_ids[None, :]).astype(BF)
    place_back = dot(place, own, 0, 0)
    taken = jnp.sum(place_back, axis=1, keepdims=True)
    free = (1.0 - taken).astype(BF)
    place_back = place_back.astype(BF)

    in_head = jnp.arange(heads)[:, None] == (jnp.arange(width) // HEAD)[None, :]
    by_head = jnp.where(in_head[:, None, :], routed[None, :, :width], 0).reshape(-1, width)
    scores = dot(by_head, mem_keys, 1, 1) * SCALE
    top = jnp.max(scores, axis=1, keepdims=True)
    exps = jnp.exp(scores - top)
    total = jnp.sum(exps, axis=1)
    part = dot(exps.astype(BF), mem_values).reshape(heads, slots, width)
    part = jnp.sum(jnp.where(in_head[:, None, :], part, 0.0), axis=0)
    tops, totals = top.reshape(heads, slots).T, total.reshape(heads, slots).T
    pad = jnp.zeros((slots, 128 - 2 * heads), F32)
    parts = exchange(jnp.concatenate([part, tops, totals, pad], axis=1), "y")
    parts = parts.reshape(window, GCAP, -1)
    tops, totals = parts[:, :, width : width + heads], parts[:, :, width + heads : width + 2 * heads]
    share = jnp.exp(tops - jnp.max(tops, axis=0))
    share = share / jnp.sum(share * totals, axis=0)
    share = jnp.dot(
        share.reshape(-1, heads), in_head.astype(F32), precision=lax.Precision.HIGHEST
    ).reshape(window, GCAP, width)
    attended = jnp.sum(parts[:, :, :width] * share, axis=0)
    here = lax.dynamic_slice_in_dim(routed, mine * GCAP, GCAP, 0)
    here_filled = lax.dynamic_slice_in_dim(filled, mine * GCAP, GCAP, 0)
    row = (here[:, width : 2 * width].astype(F32) + attended) * here_filled[:, None]
    pair = jnp.concatenate([row.astype(BF), here[:, 2 * width :]], axis=1)

    depths = lax.axis_size("z")
    copies = jnp.broadcast_to(pair[None], (depths,) + pair.shape)
    level = exchange(jnp.concatenate([copies, head_pairs(here[:, :width])], axis=2), "z")
    level = level.reshape(-1, level.shape[2])
    routed_queries = level[:, 2 * width :]
    level = level[:, : 2 * width]
    across_memory = [
        other_core(piece) for piece in jnp.split(after(own_memory, pair), PIECES, axis=1)
    ]

    bulk = [
        bulk_backward(
            core_id,
            free,
            upstream,
            queries,
            own_memory,
            across_memory[piece],
            piece,
        )
        for piece in range(PIECES)
    ]
    near = spread(after(level, free, *across_memory), "x")
    bulk_queries = jnp.concatenate([part[0] for part in bulk], axis=1)
    got = [other_core(part[2]) for part in bulk]
    near = after(near, *got)
    bulk = jnp.concatenate(
        [(part[1].astype(F32) + more.astype(F32)).astype(BF) for part, more in zip(bulk, got)], axis=1
    )
    bulk = collect(bulk, "y").astype(BF)
    far = other_core(near)
    weight_in, weight_out = w_in[0], w_out[0]
    parts_of_x = lax.axis_size("x")

    def expert(block):
        rows, grads = block[:, :width], block[:, width:]
        pre = dot(rows, weight_in, 1, 1)
        act, pullback = jax.vjp(jax.nn.gelu, pre)
        d_pre = pullback(dot(grads, weight_out, 1, 1))[0].astype(BF)
        return d_pre, dot(d_pre, rows, 0, 0), dot(act.astype(BF), grads, 0, 0), dot(d_pre, weight_in)

    _, far_in, far_out, far_back = expert(far)
    _, near_in, near_out, near_back = expert(near)
    grad_in, grad_out = (near_in + far_in).astype(BF), (near_out + far_out).astype(BF)

    back = (near_back + other_core(far_back.astype(BF)).astype(F32)).astype(BF)
    rows = back.shape[0] // parts_of_x
    back = [back.reshape(parts_of_x, rows, width), bulk.reshape(parts_of_x, -1, width)]
    back = exchange(jnp.concatenate(back, axis=1), "x")
    joined = exchange(sum_by_pairs(back), "z")
    returned, keep, send, bulk = routed_backward(
        jnp.stack([core, depth]).astype(jnp.int32),
        joined,
        level,
        routed_queries,
        own_memory,
        jnp.concatenate(across_memory, axis=1),
    )

    blocks = window * parts_of_x
    joined = join_blocks(keep, other_core(send), returned, blocks)
    joined = exchange(joined, ("y", "x"))
    rows_of_x = joined.shape[1] - returned.shape[0]
    memory = (jnp.sum(joined[:, :rows_of_x].astype(F32), axis=0) + bulk).astype(BF)
    returned = joined[:, rows_of_x:].reshape((window, parts_of_x) + returned.shape)
    returned = lax.dynamic_index_in_dim(returned, lax.axis_index("x"), 1, False)
    returned = returned.reshape(window, 2, depths, GCAP, 2 * HEAD).transpose(2, 0, 1, 3, 4)
    copies = jnp.broadcast_to(memory[None], (depths,) + memory.shape)
    joined = exchange(
        jnp.concatenate([copies, returned.reshape(depths, -1, 2 * HEAD)], axis=1), "z"
    )
    memory, returned = joined[:, :rows_of_x], rows_of(joined[:, rows_of_x:])
    returned = returned.reshape(window, 2, GCAP, width)
    moe_rows, query_rows = returned[:, 0].reshape(slots, width), returned[:, 1].reshape(slots, width)
    memory = spread(rows_of(memory), ("x", "c")).reshape(parts_of_x, 2, -1, width)
    grad_keys, grad_values = memory[:, 0].reshape(-1, width), memory[:, 1].reshape(-1, width)
    moe_grad = dot(place_back, moe_rows)
    grad_states = (upstream.astype(F32) + moe_grad).astype(BF)
    grad_queries = jnp.where(taken > 0, dot(place_back, query_rows).astype(BF), bulk_queries)
    return grad_states, grad_queries, grad_keys, grad_values, grad_in[None], grad_out[None]


def solution(mesh):
    chips = Mesh(mesh.devices.reshape(4, 16, 4, 2), DEVICES)
    rows, memory, weights = P(DEVICES, None), P("y", None), P("y", PLANE, None)
    return jax.shard_map(
        per_device,
        mesh=chips,
        in_specs=(rows, rows, memory, memory, P(DEVICES), rows, weights, weights, rows),
        out_specs=(rows, rows, memory, memory, weights, weights),
        check_vma=False,
    )
```

```python
import jax
import jax.numpy as jnp
from jax import lax
from jax.experimental import pallas as pl
from jax.experimental.pallas import tpu as pltpu
from jax.sharding import Mesh, PartitionSpec as P

HEAD = 64
GCAP = 2
PIECES = 2
SENDS = 1
SCALE = HEAD ** (-0.5)
BF, F32 = jnp.bfloat16, jnp.float32
DEVICES = ("y", "z", "x", "c")
PLANE = ("z", "x", "c")


def dot(left, right, left_dim=1, right_dim=0):
    return lax.dot_general(
        left, right, (((left_dim,), (right_dim,)), ((), ())), preferred_element_type=F32
    )


def exchange(values, axes):
    return lax.all_to_all(values, axes, split_axis=0, concat_axis=0, tiled=True)


def spread(values, axes):
    n = lax.axis_size(axes)
    copies = jnp.broadcast_to(values[None], (n,) + values.shape).reshape(
        (n * values.shape[0],) + values.shape[1:]
    )
    return exchange(copies, axes)


def collect(values, axes):
    n = lax.axis_size(axes)
    got = exchange(values, axes)
    return jnp.sum(got.reshape((n, -1) + got.shape[1:]).astype(F32), axis=0)


def join_kernel(spot_ref, keep_ref, got_ref, more_ref, ret_ref, out_ref):
    blocks = out_ref.shape[0]
    rows = keep_ref.shape[0] // blocks
    for block in range(blocks):
        part = pl.ds(block * rows, rows)
        memory = keep_ref[part].astype(F32) + got_ref[part].astype(F32)
        memory = memory + jnp.where(spot_ref[0] == block, more_ref[rows:], 0.0)
        out_ref[block, :rows] = memory.astype(BF)
        out_ref[block, rows:] = ret_ref[...]


def join_blocks(spot, keep, got, more, returned, blocks):
    vmem = pl.BlockSpec(memory_space=pltpu.VMEM)
    shape = (blocks, keep.shape[0] // blocks + returned.shape[0], keep.shape[1])
    return pl.pallas_call(
        join_kernel,
        in_specs=[pl.BlockSpec(memory_space=pltpu.SMEM)] + [vmem] * 4,
        out_specs=vmem,
        out_shape=jax.ShapeDtypeStruct(shape, BF),
    )(spot, keep, got, more, returned)


def sum_kernel(parts_ref, out_ref):
    for pair in range(out_ref.shape[0]):
        cols = slice(pair * 2 * HEAD, (pair + 1) * 2 * HEAD)
        total = parts_ref[0, :, cols].astype(F32)
        for part in range(1, parts_ref.shape[0]):
            total = total + parts_ref[part, :, cols].astype(F32)
        out_ref[pair] = total.astype(BF)


def sum_by_pairs(parts):
    vmem = pl.BlockSpec(memory_space=pltpu.VMEM)
    shape = (parts.shape[2] // (2 * HEAD), parts.shape[1], 2 * HEAD)
    return pl.pallas_call(
        sum_kernel, in_specs=[vmem], out_specs=vmem, out_shape=jax.ShapeDtypeStruct(shape, BF)
    )(parts)


def head_pairs(values):
    rows, width = values.shape
    return values.reshape(rows, width // (2 * HEAD), 2 * HEAD).transpose(1, 0, 2)


def rows_of(pairs):
    return pairs.transpose(1, 0, 2).reshape(pairs.shape[1], -1)


def after(values, *others):
    return lax.optimization_barrier((values,) + others)[0]


def other_core(values):
    return lax.ppermute(values, "c", [(0, 1), (1, 0)])


def both_heads(block):
    low = lax.broadcasted_iota(jnp.int32, block.shape, 1) < HEAD
    none = jnp.zeros_like(block)
    return jnp.concatenate([jnp.where(low, block, none), jnp.where(low, none, block)], axis=0)


def pair_backward(first, queries, grads, own, across):
    tokens = queries.shape[0]
    keys, values = jnp.where(first, own, across), jnp.where(first, across, own)
    queries, grads = both_heads(queries * BF(SCALE)), both_heads(grads)
    scores = dot(keys, queries, 1, 1)
    exps = jnp.exp(scores - jnp.max(scores, axis=0, keepdims=True))
    probs = exps * (1.0 / jnp.sum(exps, axis=0, keepdims=True))
    d_probs = dot(values, grads, 1, 1)
    centre = jnp.sum(probs * d_probs, axis=0, keepdims=True)
    d_scores = (probs * (d_probs - centre)).astype(BF)
    g_keys = dot(d_scores, queries)
    g_values = dot(probs.astype(BF), grads)
    g_queries = dot(keys, d_scores, 0, 0)
    g_queries = jnp.concatenate([g_queries[:HEAD, :tokens], g_queries[HEAD:, tokens:]], axis=0)
    keep = jnp.where(first, g_keys, g_values).astype(BF)
    send = jnp.where(first, g_values, g_keys).astype(BF)
    return (g_queries.T * SCALE).astype(BF), keep, send


def bulk_kernel(core_ref, free_ref, up_ref, q_ref, own_ref, *refs):
    across, (gq_ref, keep_ref), sends = refs[:PIECES], refs[PIECES : PIECES + 2], refs[PIECES + 2 :]
    first = core_ref[0] == 0
    free = free_ref[...]
    rows = sends[0].shape[0]
    for pair in range(q_ref.shape[1] // (2 * HEAD)):
        cols = slice(pair * 2 * HEAD, (pair + 1) * 2 * HEAD)
        gq_ref[:, cols], keep_ref[:, cols], send = pair_backward(
            first,
            q_ref[:, cols],
            up_ref[:, cols] * free,
            own_ref[:, cols],
            jnp.concatenate([ref[:, cols] for ref in across], axis=0),
        )
        for i, ref in enumerate(sends):
            ref[:, cols] = send[i * rows : (i + 1) * rows]


def bulk_backward(core, free, upstream, queries, own, across):
    tokens, width = queries.shape
    mem = own.shape[0]
    block = 512
    column = lambda n: pl.BlockSpec((n, block), lambda i: (0, i))
    outs = [tokens, mem] + [mem // SENDS] * SENDS
    got = pl.pallas_call(
        bulk_kernel,
        grid=(width // block,),
        in_specs=[
            pl.BlockSpec(memory_space=pltpu.SMEM),
            pl.BlockSpec(free.shape, lambda i: (0, 0)),
            column(tokens),
            column(tokens),
            column(mem),
        ]
        + [column(mem // PIECES)] * PIECES,
        out_specs=[column(n) for n in outs],
        out_shape=[jax.ShapeDtypeStruct((n, width), BF) for n in outs],
        cost_estimate=pl.CostEstimate(
            flops=12 * tokens * mem * width, bytes_accessed=8 * mem * width, transcendentals=0
        ),
    )(core, free, upstream, queries, own, *across)
    return got[0], got[1], got[2:]


def routed_kernel(
    spot_ref, sums_ref, up_ref, q_ref, own_ref, across_ref, ret_ref, keep_ref, send_ref, bulk_ref
):
    first = spot_ref[0] == 0
    tokens = q_ref.shape[0]
    sums = jnp.sum(sums_ref[...].astype(F32), axis=0)
    moe = sums[:tokens].astype(BF)
    bulk_ref[...] = sums[tokens:]
    grads = (up_ref[...].astype(F32) + moe.astype(F32)).astype(BF)
    g_queries, keep_ref[...], send_ref[...] = pair_backward(
        first, q_ref[...], grads, own_ref[...], across_ref[...]
    )
    ret_ref[:tokens] = moe
    ret_ref[tokens:] = g_queries


def routed_backward(spot, sums, gathered, queries, own, across):
    tokens, lanes = queries.shape
    mem, more = own.shape[0], sums.shape[1] - tokens
    whole = lambda shape: pl.BlockSpec(shape, lambda i, spot: (0,) * len(shape))
    skip = gathered.shape[1] // lanes // 2
    column = lambda n, base: pl.BlockSpec((n, lanes), lambda i, spot: (0, base + spot[1]))
    outs = [(2 * tokens, lanes), (mem, lanes), (mem, lanes), (more, lanes)]
    return pl.pallas_call(
        routed_kernel,
        grid_spec=pltpu.PrefetchScalarGridSpec(
            num_scalar_prefetch=1,
            grid=(1,),
            in_specs=[
                whole(sums.shape),
                column(tokens, skip),
                whole(queries.shape),
                column(mem, 0),
                column(mem, 0),
            ],
            out_specs=[whole(shape) for shape in outs],
        ),
        out_shape=[
            jax.ShapeDtypeStruct(shape, dtype) for shape, dtype in zip(outs, (BF, BF, BF, F32))
        ],
    )(spot, sums, gathered, queries, own, across)


def pick_kernel(core_ref, counts_ref, ids_ref, keys_ref, values_ref, *refs):
    parts, (rows_ref, place_ref, own_ref) = refs[:-3], refs[-3:]
    own_ref[...] = jnp.where(core_ref[0] == 0, keys_ref[...], values_ref[...])
    slots, tokens = place_ref.shape
    slot = lax.broadcasted_iota(jnp.int32, (slots, tokens), 0)
    expert, order = slot // GCAP, slot % GCAP
    count = jnp.zeros((slots, tokens), jnp.int32)
    for e in range(slots // GCAP):
        count = jnp.where(expert == e, counts_ref[0, e], count)
    named = ids_ref[...] == expert
    earlier = lax.broadcasted_iota(jnp.int32, (tokens, tokens), 0)
    earlier = (earlier < lax.broadcasted_iota(jnp.int32, (tokens, tokens), 1)).astype(BF)
    rank = dot(named.astype(BF), earlier).astype(jnp.int32)
    place = (named & (rank == order) & (rank < count)).astype(BF)
    place_ref[...] = place
    width = parts[0].shape[1]
    for i, part in enumerate(parts):
        rows = dot(place, part[...]).astype(BF)
        for copy in range(rows_ref.shape[0]):
            rows_ref[copy, :, i * width : (i + 1) * width] = rows
    for copy in range(rows_ref.shape[0]):
        rows_ref[copy, :, len(parts) * width :] = count.astype(F32).astype(BF)


def pick_rows(core, counts, ids, keys, values, parts, slots, copies):
    tokens, width = parts[0].shape
    vmem = pl.BlockSpec(memory_space=pltpu.VMEM)
    return pl.pallas_call(
        pick_kernel,
        in_specs=[pl.BlockSpec(memory_space=pltpu.SMEM)] * 2 + [vmem] * (3 + len(parts)),
        out_specs=[vmem] * 3,
        out_shape=[
            jax.ShapeDtypeStruct((copies, slots, len(parts) * width + tokens), BF),
            jax.ShapeDtypeStruct((slots, tokens), BF),
            jax.ShapeDtypeStruct(keys.shape, BF),
        ],
    )(core, counts, ids, keys, values, *parts)


def per_device(
    states, queries, mem_keys, mem_values, expert_ids, send_counts, w_in, w_out, upstream
):
    tokens, width = states.shape
    heads = width // HEAD
    window = lax.axis_size("y")
    slots = window * GCAP
    mine, core, depth = lax.axis_index("y"), lax.axis_index("c"), lax.axis_index("z")
    first = core == 0

    experts = jnp.arange(window, dtype=jnp.int32)
    slot_ids = jnp.arange(slots, dtype=jnp.int32)
    core_id = core.reshape(1).astype(jnp.int32)
    picked, place, own_memory = pick_rows(
        core_id,
        send_counts,
        expert_ids.reshape(1, tokens),
        mem_keys,
        mem_values,
        (queries, states, upstream),
        slots,
        window,
    )
    own_memory = lax.all_gather(own_memory, "y", axis=0, tiled=True)
    group = exchange(picked, "y").reshape(window * slots, -1)

    counts = group[:, 3 * width].reshape(window, slots)[:, ::GCAP].astype(jnp.int32)
    offsets = jnp.cumsum(counts, axis=0).astype(jnp.int32) - counts
    order = jnp.arange(GCAP, dtype=jnp.int32)
    position = offsets[:, :, None] + order
    kept = (order < counts[:, :, None]) & (position < GCAP)
    target = jnp.where(kept, experts[None, :, None] * GCAP + position, -1).reshape(-1)
    pack = (slot_ids[:, None] == target[None, :]).astype(BF)
    filled = jnp.sum(pack.astype(F32), axis=1)
    routed = dot(pack, group[:, : 3 * width]).astype(BF)
    own_target = lax.dynamic_slice_in_dim(target, mine * slots, slots, 0)
    own = (own_target[:, None] == slot_ids[None, :]).astype(BF)
    place_back = dot(place, own, 0, 0)
    taken = jnp.sum(place_back, axis=1, keepdims=True)
    free = (1.0 - taken).astype(BF)
    place_back = place_back.astype(BF)

    in_head = jnp.arange(heads)[:, None] == (jnp.arange(width) // HEAD)[None, :]
    by_head = jnp.where(in_head[:, None, :], routed[None, :, :width], 0).reshape(-1, width)
    scores = dot(by_head, mem_keys, 1, 1) * SCALE
    top = jnp.max(scores, axis=1, keepdims=True)
    exps = jnp.exp(scores - top)
    total = jnp.sum(exps, axis=1)
    part = dot(exps.astype(BF), mem_values).reshape(heads, slots, width)
    part = jnp.sum(jnp.where(in_head[:, None, :], part, 0.0), axis=0)
    tops, totals = top.reshape(heads, slots).T, total.reshape(heads, slots).T
    pad = jnp.zeros((slots, 128 - 2 * heads), F32)
    parts = exchange(jnp.concatenate([part, tops, totals, pad], axis=1), "y")
    parts = parts.reshape(window, GCAP, -1)
    tops, totals = parts[:, :, width : width + heads], parts[:, :, width + heads : width + 2 * heads]
    share = jnp.exp(tops - jnp.max(tops, axis=0))
    share = share / jnp.sum(share * totals, axis=0)
    share = jnp.dot(
        share.reshape(-1, heads), in_head.astype(F32), precision=lax.Precision.HIGHEST
    ).reshape(window, GCAP, width)
    attended = jnp.sum(parts[:, :, :width] * share, axis=0)
    here = lax.dynamic_slice_in_dim(routed, mine * GCAP, GCAP, 0)
    here_filled = lax.dynamic_slice_in_dim(filled, mine * GCAP, GCAP, 0)
    row = (here[:, width : 2 * width].astype(F32) + attended) * here_filled[:, None]
    pair = jnp.concatenate([row.astype(BF), here[:, 2 * width :]], axis=1)

    depths = lax.axis_size("z")
    copies = jnp.broadcast_to(pair[None], (depths,) + pair.shape)
    level = exchange(jnp.concatenate([copies, head_pairs(here[:, :width])], axis=2), "z")
    level = level.reshape(-1, level.shape[2])
    routed_queries = level[:, 2 * width :]
    level = level[:, : 2 * width]
    across_memory = [
        other_core(piece) for piece in jnp.split(after(own_memory, pair), PIECES, axis=0)
    ]

    bulk_queries, keep, send = bulk_backward(
        core_id, free, upstream, queries, own_memory, across_memory
    )
    near = spread(after(level, free, *across_memory), "x")
    got = [other_core(piece) for piece in send]
    bulk = (keep.astype(F32) + jnp.concatenate(got, axis=0).astype(F32)).astype(BF)
    own_rows = mem_keys.shape[0]
    blocks = [
        lax.dynamic_slice_in_dim(bulk, (mine + d) % window * own_rows, own_rows, 0)
        for d in range(window)
    ]
    moves = [[(i, (i + d) % window) for i in range(window)] for d in range(window)]
    got = [lax.ppermute(blocks[d], "y", moves[d]) for d in (1, 3)]
    far = other_core(near)
    weight_in, weight_out = w_in[0], w_out[0]
    parts_of_x = lax.axis_size("x")

    def expert(block):
        rows, grads = block[:, :width], block[:, width:]
        pre = dot(rows, weight_in, 1, 1)
        act, pullback = jax.vjp(jax.nn.gelu, pre)
        d_pre = pullback(dot(grads, weight_out, 1, 1))[0].astype(BF)
        return d_pre, dot(d_pre, rows, 0, 0), dot(act.astype(BF), grads, 0, 0), dot(d_pre, weight_in)

    _, far_in, far_out, far_back = expert(far)
    _, near_in, near_out, near_back = expert(near)
    bulk = sum(part.astype(F32) for part in blocks[:1] + [after(part, far_back) for part in got])
    bulk = jnp.stack([bulk.astype(BF), blocks[2]])
    grad_in, grad_out = (near_in + far_in).astype(BF), (near_out + far_out).astype(BF)

    back = (near_back + other_core(far_back.astype(BF)).astype(F32)).astype(BF)
    rows = back.shape[0] // parts_of_x
    bulk = bulk.reshape(2, parts_of_x, -1, width).transpose(1, 0, 2, 3)
    back = [back.reshape(parts_of_x, rows, width), bulk.reshape(parts_of_x, -1, width)]
    back = exchange(jnp.concatenate(back, axis=1), "x")
    joined = exchange(sum_by_pairs(back), "z")
    returned, keep, send, bulk = routed_backward(
        jnp.stack([core, depth]).astype(jnp.int32),
        joined,
        level,
        routed_queries,
        own_memory,
        jnp.concatenate(across_memory, axis=0),
    )

    blocks = window * parts_of_x
    spot = ((mine + 2) % window * parts_of_x + lax.axis_index("x")).reshape(1).astype(jnp.int32)
    joined = join_blocks(spot, keep, other_core(send), bulk, returned, blocks)
    joined = exchange(joined, ("y", "x"))
    rows_of_x = joined.shape[1] - returned.shape[0]
    memory = (jnp.sum(joined[:, :rows_of_x].astype(F32), axis=0) + bulk[:rows_of_x]).astype(BF)
    returned = joined[:, rows_of_x:].reshape((window, parts_of_x) + returned.shape)
    returned = lax.dynamic_index_in_dim(returned, lax.axis_index("x"), 1, False)
    returned = returned.reshape(window, 2, depths, GCAP, 2 * HEAD).transpose(2, 0, 1, 3, 4)
    copies = jnp.broadcast_to(memory[None], (depths,) + memory.shape)
    joined = exchange(
        jnp.concatenate([copies, returned.reshape(depths, -1, 2 * HEAD)], axis=1), "z"
    )
    memory, returned = joined[:, :rows_of_x], rows_of(joined[:, rows_of_x:])
    returned = returned.reshape(window, 2, GCAP, width)
    moe_rows, query_rows = returned[:, 0].reshape(slots, width), returned[:, 1].reshape(slots, width)
    memory = spread(rows_of(memory), ("x", "c")).reshape(parts_of_x, 2, -1, width)
    grad_keys, grad_values = memory[:, 0].reshape(-1, width), memory[:, 1].reshape(-1, width)
    moe_grad = dot(place_back, moe_rows)
    grad_states = (upstream.astype(F32) + moe_grad).astype(BF)
    grad_queries = jnp.where(taken > 0, dot(place_back, query_rows).astype(BF), bulk_queries)
    return grad_states, grad_queries, grad_keys, grad_values, grad_in[None], grad_out[None]


def solution(mesh):
    chips = Mesh(mesh.devices.reshape(4, 16, 4, 2), DEVICES)
    rows, memory, weights = P(DEVICES, None), P("y", None), P("y", PLANE, None)
    return jax.shard_map(
        per_device,
        mesh=chips,
        in_specs=(rows, rows, memory, memory, P(DEVICES), rows, weights, weights, rows),
        out_specs=(rows, rows, memory, memory, weights, weights),
        check_vma=False,
    )
```

```python
import jax
import jax.numpy as jnp
from jax import lax
from jax.experimental import pallas as pl
from jax.experimental.pallas import tpu as pltpu
from jax.sharding import Mesh, PartitionSpec as P

HEAD = 64
GCAP = 2
PIECES = 2
SENDS = 1
SCALE = HEAD ** (-0.5)
BF, F32 = jnp.bfloat16, jnp.float32
DEVICES = ("y", "z", "x", "c")
PLANE = ("z", "x", "c")


def dot(left, right, left_dim=1, right_dim=0):
    return lax.dot_general(
        left, right, (((left_dim,), (right_dim,)), ((), ())), preferred_element_type=F32
    )


def exchange(values, axes):
    return lax.all_to_all(values, axes, split_axis=0, concat_axis=0, tiled=True)


def spread(values, axes):
    n = lax.axis_size(axes)
    copies = jnp.broadcast_to(values[None], (n,) + values.shape).reshape(
        (n * values.shape[0],) + values.shape[1:]
    )
    return exchange(copies, axes)


def collect(values, axes):
    n = lax.axis_size(axes)
    got = exchange(values, axes)
    return jnp.sum(got.reshape((n, -1) + got.shape[1:]).astype(F32), axis=0)


def join_kernel(spot_ref, keep_ref, got_ref, more_ref, ret_ref, out_ref):
    blocks = out_ref.shape[0]
    rows = keep_ref.shape[0] // blocks
    for block in range(blocks):
        part = pl.ds(block * rows, rows)
        memory = keep_ref[part].astype(F32) + got_ref[part].astype(F32)
        memory = memory + jnp.where(spot_ref[0] == block, more_ref[rows:], 0.0)
        out_ref[block, :rows] = memory.astype(BF)
        out_ref[block, rows:] = ret_ref[...]


def join_blocks(spot, keep, got, more, returned, blocks):
    vmem = pl.BlockSpec(memory_space=pltpu.VMEM)
    shape = (blocks, keep.shape[0] // blocks + returned.shape[0], keep.shape[1])
    return pl.pallas_call(
        join_kernel,
        in_specs=[pl.BlockSpec(memory_space=pltpu.SMEM)] + [vmem] * 4,
        out_specs=vmem,
        out_shape=jax.ShapeDtypeStruct(shape, BF),
    )(spot, keep, got, more, returned)


def sum_kernel(parts_ref, out_ref):
    for pair in range(out_ref.shape[0]):
        cols = slice(pair * 2 * HEAD, (pair + 1) * 2 * HEAD)
        total = parts_ref[0, :, cols].astype(F32)
        for part in range(1, parts_ref.shape[0]):
            total = total + parts_ref[part, :, cols].astype(F32)
        out_ref[pair] = total.astype(BF)


def sum_by_pairs(parts):
    vmem = pl.BlockSpec(memory_space=pltpu.VMEM)
    shape = (parts.shape[2] // (2 * HEAD), parts.shape[1], 2 * HEAD)
    return pl.pallas_call(
        sum_kernel, in_specs=[vmem], out_specs=vmem, out_shape=jax.ShapeDtypeStruct(shape, BF)
    )(parts)


def head_pairs(values):
    rows, width = values.shape
    return values.reshape(rows, width // (2 * HEAD), 2 * HEAD).transpose(1, 0, 2)


def rows_of(pairs):
    return pairs.transpose(1, 0, 2).reshape(pairs.shape[1], -1)


def after(values, *others):
    return lax.optimization_barrier((values,) + others)[0]


def other_core(values):
    return lax.ppermute(values, "c", [(0, 1), (1, 0)])


def both_heads(block):
    low = lax.broadcasted_iota(jnp.int32, block.shape, 1) < HEAD
    none = jnp.zeros_like(block)
    return jnp.concatenate([jnp.where(low, block, none), jnp.where(low, none, block)], axis=0)


def pair_backward(first, queries, grads, own, across):
    tokens = queries.shape[0]
    keys, values = jnp.where(first, own, across), jnp.where(first, across, own)
    queries, grads = both_heads(queries * BF(SCALE)), both_heads(grads)
    scores = dot(keys, queries, 1, 1)
    exps = jnp.exp(scores - jnp.max(scores, axis=0, keepdims=True))
    probs = exps * (1.0 / jnp.sum(exps, axis=0, keepdims=True))
    d_probs = dot(values, grads, 1, 1)
    centre = jnp.sum(probs * d_probs, axis=0, keepdims=True)
    d_scores = (probs * (d_probs - centre)).astype(BF)
    g_keys = dot(d_scores, queries)
    g_values = dot(probs.astype(BF), grads)
    g_queries = dot(keys, d_scores, 0, 0)
    g_queries = jnp.concatenate([g_queries[:HEAD, :tokens], g_queries[HEAD:, tokens:]], axis=0)
    keep = jnp.where(first, g_keys, g_values).astype(BF)
    send = jnp.where(first, g_values, g_keys).astype(BF)
    return (g_queries.T * SCALE).astype(BF), keep, send


def bulk_kernel(core_ref, free_ref, up_ref, q_ref, own_ref, *refs):
    across, (gq_ref, keep_ref), sends = refs[:PIECES], refs[PIECES : PIECES + 2], refs[PIECES + 2 :]
    first = core_ref[0] == 0
    free = free_ref[...]
    rows = sends[0].shape[0]
    for pair in range(q_ref.shape[1] // (2 * HEAD)):
        cols = slice(pair * 2 * HEAD, (pair + 1) * 2 * HEAD)
        gq_ref[:, cols], keep_ref[:, cols], send = pair_backward(
            first,
            q_ref[:, cols],
            up_ref[:, cols] * free,
            own_ref[:, cols],
            jnp.concatenate([ref[:, cols] for ref in across], axis=0),
        )
        for i, ref in enumerate(sends):
            ref[:, cols] = send[i * rows : (i + 1) * rows]


def bulk_backward(core, free, upstream, queries, own, across):
    tokens, width = queries.shape
    mem = own.shape[0]
    block = 512
    column = lambda n: pl.BlockSpec((n, block), lambda i: (0, i))
    outs = [tokens, mem] + [mem // SENDS] * SENDS
    got = pl.pallas_call(
        bulk_kernel,
        grid=(width // block,),
        in_specs=[
            pl.BlockSpec(memory_space=pltpu.SMEM),
            pl.BlockSpec(free.shape, lambda i: (0, 0)),
            column(tokens),
            column(tokens),
            column(mem),
        ]
        + [column(mem // PIECES)] * PIECES,
        out_specs=[column(n) for n in outs],
        out_shape=[jax.ShapeDtypeStruct((n, width), BF) for n in outs],
        cost_estimate=pl.CostEstimate(
            flops=12 * tokens * mem * width, bytes_accessed=8 * mem * width, transcendentals=0
        ),
    )(core, free, upstream, queries, own, *across)
    return got[0], got[1], got[2:]


def routed_kernel(
    core_ref, sums_ref, up_ref, q_ref, own_ref, across_ref, ret_ref, keep_ref, send_ref, bulk_ref
):
    first = core_ref[0] == 0
    tokens = q_ref.shape[0]
    sums = jnp.sum(sums_ref[...].astype(F32), axis=0)
    moe = sums[:tokens].astype(BF)
    bulk_ref[...] = sums[tokens:]
    grads = (up_ref[...].astype(F32) + moe.astype(F32)).astype(BF)
    g_queries, keep_ref[...], send_ref[...] = pair_backward(
        first, q_ref[...], grads, own_ref[...], across_ref[...]
    )
    ret_ref[:tokens] = moe
    ret_ref[tokens:] = g_queries


def routed_backward(core, sums, upstream, queries, own, across):
    tokens, lanes = queries.shape
    mem, more = own.shape[0], sums.shape[1] - tokens
    vmem = pl.BlockSpec(memory_space=pltpu.VMEM)
    outs = [(2 * tokens, lanes), (mem, lanes), (mem, lanes), (more, lanes)]
    return pl.pallas_call(
        routed_kernel,
        in_specs=[pl.BlockSpec(memory_space=pltpu.SMEM)] + [vmem] * 5,
        out_specs=[vmem] * 4,
        out_shape=[
            jax.ShapeDtypeStruct(shape, dtype) for shape, dtype in zip(outs, (BF, BF, BF, F32))
        ],
    )(core, sums, upstream, queries, own, across)


def pick_kernel(core_ref, counts_ref, ids_ref, keys_ref, values_ref, *refs):
    parts, (rows_ref, place_ref, own_ref) = refs[:-3], refs[-3:]
    own_ref[...] = jnp.where(core_ref[0] == 0, keys_ref[...], values_ref[...])
    slots, tokens = place_ref.shape
    slot = lax.broadcasted_iota(jnp.int32, (slots, tokens), 0)
    expert, order = slot // GCAP, slot % GCAP
    count = jnp.zeros((slots, tokens), jnp.int32)
    for e in range(slots // GCAP):
        count = jnp.where(expert == e, counts_ref[0, e], count)
    named = ids_ref[...] == expert
    earlier = lax.broadcasted_iota(jnp.int32, (tokens, tokens), 0)
    earlier = (earlier < lax.broadcasted_iota(jnp.int32, (tokens, tokens), 1)).astype(BF)
    rank = dot(named.astype(BF), earlier).astype(jnp.int32)
    place = (named & (rank == order) & (rank < count)).astype(BF)
    place_ref[...] = place
    width = parts[0].shape[1]
    for i, part in enumerate(parts):
        rows = dot(place, part[...]).astype(BF)
        for copy in range(rows_ref.shape[0]):
            rows_ref[copy, :, i * width : (i + 1) * width] = rows
    for copy in range(rows_ref.shape[0]):
        rows_ref[copy, :, len(parts) * width :] = count.astype(F32).astype(BF)


def pick_rows(core, counts, ids, keys, values, parts, slots, copies):
    tokens, width = parts[0].shape
    vmem = pl.BlockSpec(memory_space=pltpu.VMEM)
    return pl.pallas_call(
        pick_kernel,
        in_specs=[pl.BlockSpec(memory_space=pltpu.SMEM)] * 2 + [vmem] * (3 + len(parts)),
        out_specs=[vmem] * 3,
        out_shape=[
            jax.ShapeDtypeStruct((copies, slots, len(parts) * width + tokens), BF),
            jax.ShapeDtypeStruct((slots, tokens), BF),
            jax.ShapeDtypeStruct(keys.shape, BF),
        ],
    )(core, counts, ids, keys, values, *parts)


def per_device(
    states, queries, mem_keys, mem_values, expert_ids, send_counts, w_in, w_out, upstream
):
    tokens, width = states.shape
    heads = width // HEAD
    window = lax.axis_size("y")
    slots = window * GCAP
    mine, core, depth = lax.axis_index("y"), lax.axis_index("c"), lax.axis_index("z")
    first = core == 0

    experts = jnp.arange(window, dtype=jnp.int32)
    slot_ids = jnp.arange(slots, dtype=jnp.int32)
    core_id = core.reshape(1).astype(jnp.int32)
    picked, place, own_memory = pick_rows(
        core_id,
        send_counts,
        expert_ids.reshape(1, tokens),
        mem_keys,
        mem_values,
        (queries, states, upstream),
        slots,
        window,
    )
    own_memory = lax.all_gather(own_memory, "y", axis=0, tiled=True)
    group = exchange(picked, "y").reshape(window * slots, -1)

    counts = group[:, 3 * width].reshape(window, slots)[:, ::GCAP].astype(jnp.int32)
    offsets = jnp.cumsum(counts, axis=0).astype(jnp.int32) - counts
    order = jnp.arange(GCAP, dtype=jnp.int32)
    position = offsets[:, :, None] + order
    kept = (order < counts[:, :, None]) & (position < GCAP)
    target = jnp.where(kept, experts[None, :, None] * GCAP + position, -1).reshape(-1)
    pack = (slot_ids[:, None] == target[None, :]).astype(BF)
    filled = jnp.sum(pack.astype(F32), axis=1)
    routed = dot(pack, group[:, : 3 * width]).astype(BF)
    own_target = lax.dynamic_slice_in_dim(target, mine * slots, slots, 0)
    own = (own_target[:, None] == slot_ids[None, :]).astype(BF)
    place_back = dot(place, own, 0, 0)
    taken = jnp.sum(place_back, axis=1, keepdims=True)
    free = (1.0 - taken).astype(BF)
    place_back = place_back.astype(BF)

    in_head = jnp.arange(heads)[:, None] == (jnp.arange(width) // HEAD)[None, :]
    by_head = jnp.where(in_head[:, None, :], routed[None, :, :width], 0).reshape(-1, width)
    scores = dot(by_head, mem_keys, 1, 1) * SCALE
    top = jnp.max(scores, axis=1, keepdims=True)
    exps = jnp.exp(scores - top)
    total = jnp.sum(exps, axis=1)
    part = dot(exps.astype(BF), mem_values).reshape(heads, slots, width)
    part = jnp.sum(jnp.where(in_head[:, None, :], part, 0.0), axis=0)
    tops, totals = top.reshape(heads, slots).T, total.reshape(heads, slots).T
    pad = jnp.zeros((slots, 128 - 2 * heads), F32)
    parts = exchange(jnp.concatenate([part, tops, totals, pad], axis=1), "y")
    parts = parts.reshape(window, GCAP, -1)
    tops, totals = parts[:, :, width : width + heads], parts[:, :, width + heads : width + 2 * heads]
    share = jnp.exp(tops - jnp.max(tops, axis=0))
    share = share / jnp.sum(share * totals, axis=0)
    share = jnp.dot(
        share.reshape(-1, heads), in_head.astype(F32), precision=lax.Precision.HIGHEST
    ).reshape(window, GCAP, width)
    attended = jnp.sum(parts[:, :, :width] * share, axis=0)
    here = lax.dynamic_slice_in_dim(routed, mine * GCAP, GCAP, 0)
    here_filled = lax.dynamic_slice_in_dim(filled, mine * GCAP, GCAP, 0)
    row = (here[:, width : 2 * width].astype(F32) + attended) * here_filled[:, None]
    pair = jnp.concatenate([row.astype(BF), here[:, 2 * width :]], axis=1)

    depths = lax.axis_size("z")
    copies = jnp.broadcast_to(pair[None], (depths,) + pair.shape)
    level = exchange(jnp.concatenate([copies, head_pairs(here[:, :width])], axis=2), "z")
    level = level.reshape(-1, level.shape[2])
    routed_queries = level[:, 2 * width :]
    level = level[:, : 2 * width]
    across_memory = [
        other_core(piece) for piece in jnp.split(after(own_memory, pair), PIECES, axis=0)
    ]

    bulk_queries, keep, send = bulk_backward(
        core_id, free, upstream, queries, own_memory, across_memory
    )
    near = spread(after(level, free, *across_memory), "x")
    got = [other_core(piece) for piece in send]
    bulk = (keep.astype(F32) + jnp.concatenate(got, axis=0).astype(F32)).astype(BF)
    own_rows = mem_keys.shape[0]
    blocks = [
        lax.dynamic_slice_in_dim(bulk, jnp.bitwise_xor(mine, d) * own_rows, own_rows, 0)
        for d in range(window)
    ]
    got = [
        lax.ppermute(blocks[d], "y", [(i, i ^ d) for i in range(window)]) for d in (1, 3)
    ]
    far = other_core(near)
    weight_in, weight_out = w_in[0], w_out[0]
    parts_of_x = lax.axis_size("x")

    def expert(block):
        rows, grads = block[:, :width], block[:, width:]
        pre = dot(rows, weight_in, 1, 1)
        act, pullback = jax.vjp(jax.nn.gelu, pre)
        d_pre = pullback(dot(grads, weight_out, 1, 1))[0].astype(BF)
        return d_pre, dot(d_pre, rows, 0, 0), dot(act.astype(BF), grads, 0, 0), dot(d_pre, weight_in)

    _, far_in, far_out, far_back = expert(far)
    _, near_in, near_out, near_back = expert(near)
    bulk = sum(part.astype(F32) for part in blocks[:1] + [after(part, far_back) for part in got])
    bulk = jnp.stack([bulk.astype(BF), blocks[2]])
    grad_in, grad_out = (near_in + far_in).astype(BF), (near_out + far_out).astype(BF)

    back = (near_back + other_core(far_back.astype(BF)).astype(F32)).astype(BF)
    rows = back.shape[0] // parts_of_x
    bulk = bulk.reshape(2, parts_of_x, -1, width).transpose(1, 0, 2, 3)
    back = [back.reshape(parts_of_x, rows, width), bulk.reshape(parts_of_x, -1, width)]
    back = exchange(jnp.concatenate(back, axis=1), "x")
    joined = exchange(sum_by_pairs(back), "z")
    column = lambda values, skip: lax.dynamic_slice_in_dim(
        values, skip + depth * 2 * HEAD, 2 * HEAD, 1
    )
    returned, keep, send, bulk = routed_backward(
        core_id,
        joined,
        column(level, width),
        routed_queries,
        column(own_memory, 0),
        jnp.concatenate([column(piece, 0) for piece in across_memory], axis=0),
    )

    blocks = window * parts_of_x
    spot = ((mine + 2) % window * parts_of_x + lax.axis_index("x")).reshape(1).astype(jnp.int32)
    joined = join_blocks(spot, keep, other_core(send), bulk, returned, blocks)
    joined = exchange(joined, ("y", "x"))
    rows_of_x = joined.shape[1] - returned.shape[0]
    memory = (jnp.sum(joined[:, :rows_of_x].astype(F32), axis=0) + bulk[:rows_of_x]).astype(BF)
    returned = joined[:, rows_of_x:].reshape((window, parts_of_x) + returned.shape)
    returned = lax.dynamic_index_in_dim(returned, lax.axis_index("x"), 1, False)
    returned = returned.reshape(window, 2, depths, GCAP, 2 * HEAD).transpose(2, 0, 1, 3, 4)
    copies = jnp.broadcast_to(memory[None], (depths,) + memory.shape)
    joined = exchange(
        jnp.concatenate([copies, returned.reshape(depths, -1, 2 * HEAD)], axis=1), "z"
    )
    memory, returned = joined[:, :rows_of_x], rows_of(joined[:, rows_of_x:])
    returned = returned.reshape(window, 2, GCAP, width)
    moe_rows, query_rows = returned[:, 0].reshape(slots, width), returned[:, 1].reshape(slots, width)
    memory = spread(rows_of(memory), ("x", "c")).reshape(parts_of_x, 2, -1, width)
    grad_keys, grad_values = memory[:, 0].reshape(-1, width), memory[:, 1].reshape(-1, width)
    moe_grad = dot(place_back, moe_rows)
    grad_states = (upstream.astype(F32) + moe_grad).astype(BF)
    grad_queries = jnp.where(taken > 0, dot(place_back, query_rows).astype(BF), bulk_queries)
    return grad_states, grad_queries, grad_keys, grad_values, grad_in[None], grad_out[None]


def solution(mesh):
    chips = Mesh(mesh.devices.reshape(4, 16, 4, 2), DEVICES)
    rows, memory, weights = P(DEVICES, None), P("y", None), P("y", PLANE, None)
    return jax.shard_map(
        per_device,
        mesh=chips,
        in_specs=(rows, rows, memory, memory, P(DEVICES), rows, weights, weights, rows),
        out_specs=(rows, rows, memory, memory, weights, weights),
        check_vma=False,
    )
```

```python
import jax
import jax.numpy as jnp
from jax import lax
from jax.experimental import pallas as pl
from jax.experimental.pallas import tpu as pltpu
from jax.sharding import Mesh, PartitionSpec as P

HEAD = 64
GCAP = 2
PIECES = 2
SENDS = 1
SCALE = HEAD ** (-0.5)
BF, F32 = jnp.bfloat16, jnp.float32
DEVICES = ("y", "z", "x", "c")
PLANE = ("z", "x", "c")


def dot(left, right, left_dim=1, right_dim=0):
    return lax.dot_general(
        left, right, (((left_dim,), (right_dim,)), ((), ())), preferred_element_type=F32
    )


def exchange(values, axes):
    return lax.all_to_all(values, axes, split_axis=0, concat_axis=0, tiled=True)


def spread(values, axes):
    n = lax.axis_size(axes)
    copies = jnp.broadcast_to(values[None], (n,) + values.shape).reshape(
        (n * values.shape[0],) + values.shape[1:]
    )
    return exchange(copies, axes)


def collect(values, axes):
    n = lax.axis_size(axes)
    got = exchange(values, axes)
    return jnp.sum(got.reshape((n, -1) + got.shape[1:]).astype(F32), axis=0)


def join_kernel(spot_ref, keep_ref, got_ref, more_ref, ret_ref, out_ref):
    blocks = out_ref.shape[0]
    rows = keep_ref.shape[0] // blocks
    for block in range(blocks):
        part = pl.ds(block * rows, rows)
        memory = keep_ref[part].astype(F32) + got_ref[part].astype(F32)
        memory = memory + jnp.where(spot_ref[0] == block, more_ref[rows:], 0.0)
        out_ref[block, :rows] = memory.astype(BF)
        out_ref[block, rows:] = ret_ref[...]


def join_blocks(spot, keep, got, more, returned, blocks):
    vmem = pl.BlockSpec(memory_space=pltpu.VMEM)
    shape = (blocks, keep.shape[0] // blocks + returned.shape[0], keep.shape[1])
    return pl.pallas_call(
        join_kernel,
        in_specs=[pl.BlockSpec(memory_space=pltpu.SMEM)] + [vmem] * 4,
        out_specs=vmem,
        out_shape=jax.ShapeDtypeStruct(shape, BF),
    )(spot, keep, got, more, returned)


def sum_kernel(parts_ref, out_ref):
    for pair in range(out_ref.shape[0]):
        cols = slice(pair * 2 * HEAD, (pair + 1) * 2 * HEAD)
        total = parts_ref[0, :, cols].astype(F32)
        for part in range(1, parts_ref.shape[0]):
            total = total + parts_ref[part, :, cols].astype(F32)
        out_ref[pair] = total.astype(BF)


def sum_by_pairs(parts):
    vmem = pl.BlockSpec(memory_space=pltpu.VMEM)
    shape = (parts.shape[2] // (2 * HEAD), parts.shape[1], 2 * HEAD)
    return pl.pallas_call(
        sum_kernel, in_specs=[vmem], out_specs=vmem, out_shape=jax.ShapeDtypeStruct(shape, BF)
    )(parts)


def head_pairs(values):
    rows, width = values.shape
    return values.reshape(rows, width // (2 * HEAD), 2 * HEAD).transpose(1, 0, 2)


def rows_of(pairs):
    return pairs.transpose(1, 0, 2).reshape(pairs.shape[1], -1)


def after(values, *others):
    return lax.optimization_barrier((values,) + others)[0]


def other_core(values):
    return lax.ppermute(values, "c", [(0, 1), (1, 0)])


def both_heads(block):
    low = lax.broadcasted_iota(jnp.int32, block.shape, 1) < HEAD
    none = jnp.zeros_like(block)
    return jnp.concatenate([jnp.where(low, block, none), jnp.where(low, none, block)], axis=0)


def pair_backward(first, queries, grads, own, across):
    tokens = queries.shape[0]
    keys, values = jnp.where(first, own, across), jnp.where(first, across, own)
    queries, grads = both_heads(queries * BF(SCALE)), both_heads(grads)
    scores = dot(keys, queries, 1, 1)
    exps = jnp.exp(scores - jnp.max(scores, axis=0, keepdims=True))
    probs = exps * (1.0 / jnp.sum(exps, axis=0, keepdims=True))
    d_probs = dot(values, grads, 1, 1)
    centre = jnp.sum(probs * d_probs, axis=0, keepdims=True)
    d_scores = (probs * (d_probs - centre)).astype(BF)
    g_keys = dot(d_scores, queries)
    g_values = dot(probs.astype(BF), grads)
    g_queries = dot(keys, d_scores, 0, 0)
    g_queries = jnp.concatenate([g_queries[:HEAD, :tokens], g_queries[HEAD:, tokens:]], axis=0)
    keep = jnp.where(first, g_keys, g_values).astype(BF)
    send = jnp.where(first, g_values, g_keys).astype(BF)
    return (g_queries.T * SCALE).astype(BF), keep, send


def bulk_kernel(core_ref, free_ref, up_ref, q_ref, own_ref, *refs):
    across, (gq_ref, keep_ref), sends = refs[:PIECES], refs[PIECES : PIECES + 2], refs[PIECES + 2 :]
    first = core_ref[0] == 0
    free = free_ref[...]
    rows = sends[0].shape[0]
    for pair in range(q_ref.shape[1] // (2 * HEAD)):
        cols = slice(pair * 2 * HEAD, (pair + 1) * 2 * HEAD)
        gq_ref[:, cols], keep_ref[:, cols], send = pair_backward(
            first,
            q_ref[:, cols],
            up_ref[:, cols] * free,
            own_ref[:, cols],
            jnp.concatenate([ref[:, cols] for ref in across], axis=0),
        )
        for i, ref in enumerate(sends):
            ref[:, cols] = send[i * rows : (i + 1) * rows]


def bulk_backward(core, free, upstream, queries, own, across):
    tokens, width = queries.shape
    mem = own.shape[0]
    block = 512
    column = lambda n: pl.BlockSpec((n, block), lambda i: (0, i))
    outs = [tokens, mem] + [mem // SENDS] * SENDS
    got = pl.pallas_call(
        bulk_kernel,
        grid=(width // block,),
        in_specs=[
            pl.BlockSpec(memory_space=pltpu.SMEM),
            pl.BlockSpec(free.shape, lambda i: (0, 0)),
            column(tokens),
            column(tokens),
            column(mem),
        ]
        + [column(mem // PIECES)] * PIECES,
        out_specs=[column(n) for n in outs],
        out_shape=[jax.ShapeDtypeStruct((n, width), BF) for n in outs],
        cost_estimate=pl.CostEstimate(
            flops=12 * tokens * mem * width, bytes_accessed=8 * mem * width, transcendentals=0
        ),
    )(core, free, upstream, queries, own, *across)
    return got[0], got[1], got[2:]


def routed_kernel(
    core_ref, sums_ref, up_ref, q_ref, own_ref, across_ref, ret_ref, keep_ref, send_ref, bulk_ref
):
    first = core_ref[0] == 0
    tokens = q_ref.shape[0]
    sums = jnp.sum(sums_ref[...].astype(F32), axis=0)
    moe = sums[:tokens].astype(BF)
    bulk_ref[...] = sums[tokens:]
    grads = (up_ref[...].astype(F32) + moe.astype(F32)).astype(BF)
    g_queries, keep_ref[...], send_ref[...] = pair_backward(
        first, q_ref[...], grads, own_ref[...], across_ref[...]
    )
    ret_ref[:tokens] = moe
    ret_ref[tokens:] = g_queries


def routed_backward(core, sums, upstream, queries, own, across):
    tokens, lanes = queries.shape
    mem, more = own.shape[0], sums.shape[1] - tokens
    vmem = pl.BlockSpec(memory_space=pltpu.VMEM)
    outs = [(2 * tokens, lanes), (mem, lanes), (mem, lanes), (more, lanes)]
    return pl.pallas_call(
        routed_kernel,
        in_specs=[pl.BlockSpec(memory_space=pltpu.SMEM)] + [vmem] * 5,
        out_specs=[vmem] * 4,
        out_shape=[
            jax.ShapeDtypeStruct(shape, dtype) for shape, dtype in zip(outs, (BF, BF, BF, F32))
        ],
    )(core, sums, upstream, queries, own, across)


def pick_kernel(
    core_ref, counts_ref, ids_ref, keys_ref, values_ref, q_ref, states_ref, up_ref,
    rows_ref, local_ref, place_ref, own_ref,
):
    own_ref[...] = jnp.where(core_ref[0] == 0, keys_ref[...], values_ref[...])
    slots, tokens = place_ref.shape
    slot = lax.broadcasted_iota(jnp.int32, (slots, tokens), 0)
    expert, order = slot // GCAP, slot % GCAP
    count = jnp.zeros((slots, tokens), jnp.int32)
    for e in range(slots // GCAP):
        count = jnp.where(expert == e, counts_ref[0, e], count)
    named = ids_ref[...] == expert
    earlier = lax.broadcasted_iota(jnp.int32, (tokens, tokens), 0)
    earlier = (earlier < lax.broadcasted_iota(jnp.int32, (tokens, tokens), 1)).astype(BF)
    rank = dot(named.astype(BF), earlier).astype(jnp.int32)
    place = (named & (rank == order) & (rank < count)).astype(BF)
    place_ref[...] = place
    width = q_ref.shape[1]
    rows = dot(place, q_ref[...]).astype(BF)
    for copy in range(rows_ref.shape[0]):
        rows_ref[copy, :, :width] = rows
        rows_ref[copy, :, width:] = count.astype(F32).astype(BF)
    local_ref[:, :width] = dot(place, states_ref[...]).astype(BF)
    local_ref[:, width:] = dot(place, up_ref[...]).astype(BF)


def pick_rows(core, counts, ids, keys, values, parts, slots, copies):
    tokens, width = parts[0].shape
    vmem = pl.BlockSpec(memory_space=pltpu.VMEM)
    return pl.pallas_call(
        pick_kernel,
        in_specs=[pl.BlockSpec(memory_space=pltpu.SMEM)] * 2 + [vmem] * (3 + len(parts)),
        out_specs=[vmem] * 4,
        out_shape=[
            jax.ShapeDtypeStruct((copies, slots, width + tokens), BF),
            jax.ShapeDtypeStruct((slots, 2 * width), BF),
            jax.ShapeDtypeStruct((slots, tokens), BF),
            jax.ShapeDtypeStruct(keys.shape, BF),
        ],
    )(core, counts, ids, keys, values, *parts)


def per_device(
    states, queries, mem_keys, mem_values, expert_ids, send_counts, w_in, w_out, upstream
):
    tokens, width = states.shape
    heads = width // HEAD
    window = lax.axis_size("y")
    slots = window * GCAP
    mine, core, depth = lax.axis_index("y"), lax.axis_index("c"), lax.axis_index("z")
    first = core == 0

    experts = jnp.arange(window, dtype=jnp.int32)
    slot_ids = jnp.arange(slots, dtype=jnp.int32)
    core_id = core.reshape(1).astype(jnp.int32)
    picked, local, place, own_memory = pick_rows(
        core_id,
        send_counts,
        expert_ids.reshape(1, tokens),
        mem_keys,
        mem_values,
        (queries, states, upstream),
        slots,
        window,
    )
    own_memory = lax.all_gather(own_memory, "y", axis=0, tiled=True)
    group = exchange(picked, "y").reshape(window * slots, -1)

    counts = group[:, width].reshape(window, slots)[:, ::GCAP].astype(jnp.int32)
    offsets = jnp.cumsum(counts, axis=0).astype(jnp.int32) - counts
    order = jnp.arange(GCAP, dtype=jnp.int32)
    position = offsets[:, :, None] + order
    kept = (order < counts[:, :, None]) & (position < GCAP)
    target = jnp.where(kept, experts[None, :, None] * GCAP + position, -1).reshape(-1)
    pack = (slot_ids[:, None] == target[None, :]).astype(BF)
    filled = jnp.sum(pack.astype(F32), axis=1)
    routed = dot(pack, group[:, :width]).astype(BF)
    own_target = lax.dynamic_slice_in_dim(target, mine * slots, slots, 0)
    own = (own_target[:, None] == slot_ids[None, :]).astype(BF)
    local = dot(own, local, 0, 0)
    place_back = dot(place, own, 0, 0)
    taken = jnp.sum(place_back, axis=1, keepdims=True)
    free = jnp.broadcast_to((1.0 - taken).astype(BF), (tokens, 2 * HEAD))
    place_back = place_back.astype(BF)

    in_head = jnp.arange(heads)[:, None] == (jnp.arange(width) // HEAD)[None, :]
    by_head = jnp.where(in_head[:, None, :], routed[None], 0).reshape(-1, width)
    scores = dot(by_head, mem_keys, 1, 1) * SCALE
    top = jnp.max(scores, axis=1, keepdims=True)
    exps = jnp.exp(scores - top)
    total = jnp.sum(exps, axis=1)
    part = dot(exps.astype(BF), mem_values).reshape(heads, slots, width)
    part = jnp.sum(jnp.where(in_head[:, None, :], part, 0.0), axis=0)
    tops, totals = top.reshape(heads, slots).T, total.reshape(heads, slots).T
    pad = jnp.zeros((slots, 128 - 2 * heads), F32)
    parts = exchange(jnp.concatenate([part, tops, totals, pad, local], axis=1), "y")
    parts = parts.reshape(window, GCAP, -1)
    tops, totals = parts[:, :, width : width + heads], parts[:, :, width + heads : width + 2 * heads]
    share = jnp.exp(tops - jnp.max(tops, axis=0))
    share = share / jnp.sum(share * totals, axis=0)
    share = jnp.dot(
        share.reshape(-1, heads), in_head.astype(F32), precision=lax.Precision.HIGHEST
    ).reshape(window, GCAP, width)
    attended = jnp.sum(parts[:, :, :width] * share, axis=0)
    local = jnp.sum(parts[:, :, width + 128 :], axis=0)
    here = lax.dynamic_slice_in_dim(routed, mine * GCAP, GCAP, 0)
    here_filled = lax.dynamic_slice_in_dim(filled, mine * GCAP, GCAP, 0)
    row = (local[:, :width] + attended) * here_filled[:, None]
    pair = jnp.concatenate([row, local[:, width:]], axis=1).astype(BF)

    depths = lax.axis_size("z")
    copies = jnp.broadcast_to(pair[None], (depths,) + pair.shape)
    level = exchange(jnp.concatenate([copies, head_pairs(here)], axis=2), "z")
    level = level.reshape(-1, level.shape[2])
    routed_queries = level[:, 2 * width :]
    level = level[:, : 2 * width]
    across_memory = [
        other_core(piece) for piece in jnp.split(after(own_memory, pair), PIECES, axis=0)
    ]

    bulk_queries, keep, send = bulk_backward(
        core_id, free, upstream, queries, own_memory, across_memory
    )
    near = spread(after(level, free, *across_memory), "x")
    got = [other_core(piece) for piece in send]
    bulk = (keep.astype(F32) + jnp.concatenate(got, axis=0).astype(F32)).astype(BF)
    own_rows = mem_keys.shape[0]
    blocks = [
        lax.dynamic_slice_in_dim(bulk, jnp.bitwise_xor(mine, d) * own_rows, own_rows, 0)
        for d in range(window)
    ]
    got = [
        lax.ppermute(blocks[d], "y", [(i, i ^ d) for i in range(window)]) for d in (1, 3)
    ]
    far = other_core(near)
    weight_in, weight_out = w_in[0], w_out[0]
    parts_of_x = lax.axis_size("x")

    def expert(block):
        rows, grads = block[:, :width], block[:, width:]
        pre = dot(rows, weight_in, 1, 1)
        act, pullback = jax.vjp(jax.nn.gelu, pre)
        d_pre = pullback(dot(grads, weight_out, 1, 1))[0].astype(BF)
        return d_pre, dot(d_pre, rows, 0, 0), dot(act.astype(BF), grads, 0, 0), dot(d_pre, weight_in)

    _, far_in, far_out, far_back = expert(far)
    _, near_in, near_out, near_back = expert(near)
    bulk = sum(part.astype(F32) for part in blocks[:1] + [after(part, far_back) for part in got])
    bulk = jnp.stack([bulk.astype(BF), blocks[2]])
    grad_in, grad_out = (near_in + far_in).astype(BF), (near_out + far_out).astype(BF)

    back = (near_back + other_core(far_back.astype(BF)).astype(F32)).astype(BF)
    rows = back.shape[0] // parts_of_x
    bulk = bulk.reshape(2, parts_of_x, -1, width).transpose(1, 0, 2, 3)
    back = [back.reshape(parts_of_x, rows, width), bulk.reshape(parts_of_x, -1, width)]
    back = exchange(jnp.concatenate(back, axis=1), "x")
    joined = exchange(sum_by_pairs(back), "z")
    column = lambda values, skip: lax.dynamic_slice_in_dim(
        values, skip + depth * 2 * HEAD, 2 * HEAD, 1
    )
    returned, keep, send, bulk = routed_backward(
        core_id,
        joined,
        column(level, width),
        routed_queries,
        column(own_memory, 0),
        jnp.concatenate([column(piece, 0) for piece in across_memory], axis=0),
    )

    blocks = window * parts_of_x
    spot = ((mine + 2) % window * parts_of_x + lax.axis_index("x")).reshape(1).astype(jnp.int32)
    joined = join_blocks(spot, keep, other_core(send), bulk, returned, blocks)
    joined = exchange(joined, ("y", "x"))
    rows_of_x = joined.shape[1] - returned.shape[0]
    memory = (jnp.sum(joined[:, :rows_of_x].astype(F32), axis=0) + bulk[:rows_of_x]).astype(BF)
    returned = joined[:, rows_of_x:].reshape((window, parts_of_x) + returned.shape)
    returned = lax.dynamic_index_in_dim(returned, lax.axis_index("x"), 1, False)
    returned = returned.reshape(window, 2, depths, GCAP, 2 * HEAD).transpose(2, 0, 1, 3, 4)
    copies = jnp.broadcast_to(memory[None], (depths,) + memory.shape)
    joined = exchange(
        jnp.concatenate([copies, returned.reshape(depths, -1, 2 * HEAD)], axis=1), "z"
    )
    memory, returned = joined[:, :rows_of_x], rows_of(joined[:, rows_of_x:])
    returned = returned.reshape(window, 2, GCAP, width)
    moe_rows, query_rows = returned[:, 0].reshape(slots, width), returned[:, 1].reshape(slots, width)
    memory = spread(rows_of(memory), ("x", "c")).reshape(parts_of_x, 2, -1, width)
    grad_keys, grad_values = memory[:, 0].reshape(-1, width), memory[:, 1].reshape(-1, width)
    moe_grad = dot(place_back, moe_rows)
    grad_states = (upstream.astype(F32) + moe_grad).astype(BF)
    grad_queries = jnp.where(taken > 0, dot(place_back, query_rows).astype(BF), bulk_queries)
    return grad_states, grad_queries, grad_keys, grad_values, grad_in[None], grad_out[None]


def solution(mesh):
    chips = Mesh(mesh.devices.reshape(4, 16, 4, 2), DEVICES)
    rows, memory, weights = P(DEVICES, None), P("y", None), P("y", PLANE, None)
    return jax.shard_map(
        per_device,
        mesh=chips,
        in_specs=(rows, rows, memory, memory, P(DEVICES), rows, weights, weights, rows),
        out_specs=(rows, rows, memory, memory, weights, weights),
        check_vma=False,
    )
```
